768 devices in a mesh: seq: 96 (over z, y), head: 8 (over x, core).
Axes of the slice: x: 4, y: 8, z: 12, core: 2. Of those that a mesh axis runs over, the one named last changes fastest.
Arguments:
- hidden: bfloat16 [27648, 6144], P('seq', 'head'), may hold values from -4 to 4
- upstream: bfloat16 [27648, 6144], P('seq', 'head'), may hold values from -6 to 6
- w_query: bfloat16 [8, 6144, 128], P('head'), may hold values from -0.0390625 to 0.0390625
- w_key: bfloat16 [8, 6144, 128], P('head'), may hold values from -0.078125 to 0.078125
- w_value: bfloat16 [8, 6144, 128], P('head'), may hold values from -0.078125 to 0.078125
- w_output: bfloat16 [8, 128, 6144], P('head'), may hold values from -0.5 to 0.5
- selected: int32 [8, 3456], replicated, may hold values from 0 to 287, as said below
- select_count: int32 [8, 96], replicated, may hold values from 1 to 36, as said below
Outputs:
- grad_hidden: bfloat16 [27648, 6144], P('seq', 'head')
- grad_query: float32 [8, 6144, 128], P('head', 'seq')
The draws below stay inside these ranges and needn't reach their ends.
Inputs may be any that keep to these rules, and one draw needn't show every extreme that they name: `selected`: for each head h and block b, entries b * 36 to b * 36 + select_count[h, b] - 1 are distinct and ascending; the remaining entries of the block are 0. `select_count`: every head has some block with 36 used slots.
All inputs are finite; a program needn't handle non-finite values.
Results may differ from the reference program's by a relative error of at most 0.02.
Values may be sent and summed in bfloat16 or wider, within the bound.
No kernel may reach another device: no remote copies, remote signals or barrier semaphores. Data moves between devices by JAX's collectives and lax.ppermute only.
A program may use at most 64 MiB of HBM per device.

```python
import jax
import jax.numpy as jnp
from jax import lax

D = 6144
HD = 128
TOK_DEV = 288
CAP = 36
HEADS = 8
SEQLEN = 27648
N_SEQ = 96


def selection_tables(key):
    key_limit, key_raw, key_full, key_order = jax.random.split(key, 4)
    limit = jax.random.randint(key_limit, (HEADS, 1), max(CAP // 4, 1), CAP + 1)
    raw_counts = jax.random.randint(key_raw, (HEADS, N_SEQ), 0, 1 << 20)
    counts = 1 + raw_counts % limit
    full_block = jax.random.randint(key_full, (HEADS, 1), 0, N_SEQ)
    counts = jnp.where(jnp.arange(N_SEQ)[None, :] == full_block, CAP, counts).astype(jnp.int32)
    ranks = jax.random.randint(key_order, (HEADS, N_SEQ, TOK_DEV), 0, 1 << 20) * TOK_DEV + jnp.arange(TOK_DEV)[None, None, :]
    order = jnp.argsort(ranks, axis=-1)[..., :CAP]
    keep = jnp.arange(CAP)[None, None, :] < counts[..., None]
    marked = jnp.sort(jnp.where(keep, order, TOK_DEV), axis=-1)
    chosen = jnp.where(marked == TOK_DEV, 0, marked)
    return (chosen.reshape(HEADS, N_SEQ * CAP).astype(jnp.int32), counts)


def draw_selected(key, part):
    return selection_tables(key)[0]


def draw_select_count(key, part):
    return selection_tables(key)[1]


def block_levels(stream_key, extent, cuts, smallest, high):
    loudness, own = 1.0, jax.random.fold_in(stream_key, 6)
    for axis_at, parts in cuts:
        steps = jnp.exp(jax.random.uniform(jax.random.fold_in(own, axis_at), (parts,), jnp.float32, smallest / len(cuts), high / len(cuts)))
        loudness = loudness * jnp.repeat(steps, extent[axis_at] // parts).reshape([-1 if axis == axis_at else 1 for axis in range(len(extent))])
    return loudness


def bell_draw(stream_key, dims, scale, bound, shards=(), kind=jnp.bfloat16):
    level = block_levels(stream_key, dims, shards, -0.22, 0.18) if shards else 1.0
    values = jax.random.normal(stream_key, dims, jnp.float32) * scale * level
    return jnp.minimum(jnp.maximum(values, -bound), bound).astype(kind)


def setup_inputs(seed: int = 0) -> dict:
    seeds = jax.random.split(jax.random.key(seed), 9)
    hidden = bell_draw(seeds[0], (SEQLEN, D), 1.0, 4.0, ((0, 96), (1, 8)))
    upstream = bell_draw(seeds[1], (SEQLEN, D), 1.0, 6.0, ((0, 96), (1, 8)))
    w_query = bell_draw(seeds[2], (HEADS, D, HD), (4 * D) ** -0.5, 0.0390625, ((0, 8),))
    w_key = bell_draw(seeds[3], (HEADS, D, HD), D ** -0.5, 0.078125, ((0, 8),))
    w_value = bell_draw(seeds[4], (HEADS, D, HD), D ** -0.5, 0.078125, ((0, 8),))
    w_output = bell_draw(seeds[5], (HEADS, HD, D), HD ** -0.5, 0.5, ((0, 8),))
    selected = draw_selected(jax.random.fold_in(seeds[8], 71), 0)
    select_count = draw_select_count(jax.random.fold_in(seeds[8], 71), 0)
    return {"hidden": hidden, "upstream": upstream, "w_query": w_query, "w_key": w_key, "w_value": w_value, "w_output": w_output, "selected": selected, "select_count": select_count}


def reference(hidden, upstream, w_query, w_key, w_value, w_output, selected, select_count):
    slots = N_SEQ * CAP
    score_scale = HD ** -0.5
    slot_ids = jnp.arange(slots, dtype=jnp.int32)
    block_ids = slot_ids // CAP

    def one_head(inputs):
        sel_row, count_row, weight_q, weight_k, weight_v, weight_o = inputs
        positions = block_ids * TOK_DEV + sel_row
        live_slot = (slot_ids % CAP) < count_row[block_ids]
        rows_in = hidden[positions]
        rows_up = upstream[positions]
        queries = jnp.dot(rows_in, weight_q, preferred_element_type=jnp.float32).astype(jnp.bfloat16)
        keys_all = jnp.dot(rows_in, weight_k, preferred_element_type=jnp.float32).astype(jnp.bfloat16)
        values_all = jnp.dot(rows_in, weight_v, preferred_element_type=jnp.float32).astype(jnp.bfloat16)
        grad_attn = jnp.where(live_slot[:, None], jnp.dot(rows_up, weight_o.T, preferred_element_type=jnp.float32), 0.0).astype(jnp.bfloat16)
        allowed = live_slot[:, None] & live_slot[None, :] & (positions[None, :] <= positions[:, None])
        scores = jnp.dot(queries, keys_all.T, preferred_element_type=jnp.float32) * score_scale
        total = jnp.sum(jnp.where(allowed, jnp.exp(scores), 0.0), axis=-1) + jnp.where(live_slot, 0.0, 1.0)
        log_total = jnp.log(total)
        probs = jnp.where(allowed, jnp.exp(scores - log_total[:, None]), 0.0)
        probs_b = probs.astype(jnp.bfloat16)
        attended = jnp.dot(probs_b, values_all, preferred_element_type=jnp.float32).astype(jnp.bfloat16)
        delta = jnp.sum(grad_attn.astype(jnp.float32) * attended.astype(jnp.float32), axis=-1)
        grad_probs = jnp.dot(grad_attn, values_all.T, preferred_element_type=jnp.float32)
        grad_scores = (probs * (grad_probs - delta[:, None])).astype(jnp.bfloat16)
        grad_q = (jnp.dot(grad_scores, keys_all, preferred_element_type=jnp.float32) * score_scale).astype(jnp.bfloat16)
        grad_k = (jnp.dot(grad_scores.T, queries, preferred_element_type=jnp.float32) * score_scale).astype(jnp.bfloat16)
        grad_v = jnp.dot(probs_b.T, grad_attn, preferred_element_type=jnp.float32).astype(jnp.bfloat16)
        grad_rows = (jnp.dot(grad_q, weight_q.T, preferred_element_type=jnp.float32)
                     + jnp.dot(grad_k, weight_k.T, preferred_element_type=jnp.float32)
                     + jnp.dot(grad_v, weight_v.T, preferred_element_type=jnp.float32))
        grad_rows = jnp.where(live_slot[:, None], grad_rows, 0.0)
        weight_sum = jnp.dot(rows_in.T, grad_q, preferred_element_type=jnp.float32)
        return grad_rows, weight_sum

    rows_grad, weight_grads = lax.map(one_head, (selected, select_count, w_query, w_key, w_value, w_output))
    all_positions = (block_ids * TOK_DEV)[None, :] + selected
    grad_hidden = jnp.zeros((N_SEQ * TOK_DEV, D), jnp.float32).at[all_positions.reshape(-1)].add(rows_grad.reshape(-1, D))
    return (grad_hidden.astype(jnp.bfloat16), weight_grads)
```

```python
import functools

import jax
import jax.numpy as jnp
from jax import lax
from jax.experimental import pallas as pl
from jax.experimental.pallas import tpu as pltpu
from jax.sharding import Mesh, PartitionSpec as P

NY = 8
SLOT = 48
NEG = -1e30
BF = jnp.bfloat16
F32 = jnp.float32
VMEM = pl.BlockSpec(memory_space=pltpu.VMEM)
SMEM = pl.BlockSpec(memory_space=pltpu.SMEM)
NN = (((1,), (0,)), ((), ()))
NT = (((1,), (1,)), ((), ()))
TN = (((0,), (0,)), ((), ()))


def mm(a, b, dims=NN):
    return lax.dot_general(a, b, dims, preferred_element_type=F32)


def call(kernel, outs, args, specs, scratch=(), limit=20):
    return pl.pallas_call(
        kernel,
        out_shape=outs,
        in_specs=specs,
        out_specs=jax.tree.map(lambda _: VMEM, outs),
        scratch_shapes=list(scratch),
        compiler_params=pltpu.CompilerParams(vmem_limit_bytes=limit << 20),
    )(*args)


def pick_kernel(sel_ref, hid_ref, up_ref, out_ref):
    heads, rows, cols = out_ref.shape
    toks = hid_ref.shape[0]
    sel_t = sel_ref[...].astype(F32).T
    target = jnp.concatenate([sel_t[:rows, h : h + 1] for h in range(heads)], axis=0)
    target = target.astype(jnp.int32)
    lane = lax.broadcasted_iota(jnp.int32, (heads * rows, 2 * toks), 1)
    onehot = jnp.where(lane == target, 1.0, 0.0).astype(BF)
    table = jnp.concatenate([hid_ref[...], up_ref[...]], axis=0)
    out_ref[...] = mm(onehot, table).reshape(heads, rows, cols).astype(BF)


def project_kernel(
    idx_ref, cnt_ref, r_ref, wq_ref, wk_ref, wv_ref, wo_ref, y_ref, z_ref, g_acc
):
    heads, rows, cols = r_ref.shape
    cap, hd = rows // 2, wq_ref.shape[1]
    q = k = v = jnp.zeros((SLOT, hd), F32)
    g = jnp.zeros((rows, hd), F32)
    for c in range(heads):
        part = pl.ds(c * cols, cols)
        x = r_ref[c]
        q = q + mm(x[:SLOT], wq_ref[part, :])
        k = k + mm(x[:SLOT], wk_ref[part, :])
        v = v + mm(x[:SLOT], wv_ref[part, :])
        g = g + mm(x, wo_ref[:, part], NT)
    g_acc[...] = g
    g = g_acc[cap:, :]
    count = cnt_ref[idx_ref[2], idx_ref[0] * NY + idx_ref[1]]
    row = lax.broadcasted_iota(jnp.int32, (cap, hd), 0)
    g = jnp.where(row < count, g, 0.0).astype(BF)
    q, k, v = (a.astype(BF)[:cap] for a in (q, k, v))
    for i in range(y_ref.shape[0]):
        y_ref[i, :, :hd] = q
        y_ref[i, :, hd:] = g
    nz = z_ref.shape[0]
    piece = heads * cols // nz
    for i in range(nz):
        z_ref[i, :, :hd] = k
        z_ref[i, :, hd : 2 * hd] = v
        at, left, put = i * piece, piece, 2 * hd
        while left:
            c, off = at // cols, at % cols
            n = min(left, cols - off)
            z_ref[i, :, put : put + n] = r_ref[c, :cap, off : off + n]
            at, left, put = at + n, left - n, put + n


def padded(pad_ref, ref, lo, hi):
    n, cap = ref.shape[0], ref.shape[1]
    w = hi - lo
    pad_ref[:, SLOT - 16 :, :] = jnp.zeros((n, 16, w), BF)
    for i in range(n):
        pad_ref[i, :cap, :] = ref[i, :, lo:hi]
    return pad_ref[...].reshape(n * SLOT, w)


def orders(idx_ref, cnt_ref, nz, axis_q):
    z, y, h = idx_ref[0], idx_ref[1], idx_ref[2]

    def one(n, axis, block_of, dead):
        shape = (n * SLOT, 1) if axis == 0 else (1, n * SLOT)
        at = lax.broadcasted_iota(jnp.int32, shape, axis)
        out = jnp.full(shape, dead, jnp.int32)
        for i in range(n):
            b = block_of(i)
            c = at - i * SLOT
            live = (c >= 0) & (c < cnt_ref[h, b])
            out = jnp.where(live, c + b * SLOT, out)
        return out

    order_q = one(NY, axis_q, lambda i: z * NY + i, -1)
    order_k = one(nz, 1 - axis_q, lambda i: i * NY + y, 1 << 30)
    return order_q, order_k


def split(x):
    hi = x.astype(BF).astype(F32)
    return hi, x - hi


def partial_kernel(scale, idx_ref, cnt_ref, qg_ref, kv_ref, out_ref, qg_pad, kv_pad):
    nz, hd = kv_ref.shape[0], qg_ref.shape[2] // 2
    qg = padded(qg_pad, qg_ref, 0, 2 * hd)
    kv = padded(kv_pad, kv_ref, 0, 2 * hd)
    q, g, k, v = qg[:, :hd], qg[:, hd:], kv[:, :hd], kv[:, hd:]
    order_q, order_k = orders(idx_ref, cnt_ref, nz, 0)
    allowed = order_k <= order_q
    s = jnp.where(allowed, mm(q, k, NT) * scale, NEG)
    top = jnp.max(s, axis=1, keepdims=True)
    top = (top + jnp.abs(top) * (2.0**-7)).astype(BF).astype(F32)
    e = jnp.where(allowed, jnp.exp(s - top), 0.0)
    total = jnp.sum(e, axis=1, keepdims=True)
    p = e * (1.0 / jnp.where(total > 0.0, total, 1.0))
    gp = mm(g, v, NT)
    delta = jnp.sum(p * gp, axis=1, keepdims=True)
    p_b = p.astype(BF)
    a = mm((p * (gp - delta)).astype(BF), k) * scale
    b = mm(p_b, k) * scale
    t_hi, t_lo = split(total)
    d_hi, d_lo = split(delta)
    rows = q.shape[0]
    lane = lax.broadcasted_iota(jnp.int32, (rows, hd), 1)
    stats = jnp.zeros((rows, hd), F32)
    for i, col in enumerate((top, t_hi, t_lo, d_hi, d_lo)):
        stats = jnp.where(lane == i, col, stats)
    flat = stats.T[:16, :].astype(BF)
    own = jnp.concatenate([a, b, stats], axis=1).astype(BF)
    for i in range(NY):
        out_ref[i, :SLOT, :] = own[i * SLOT : (i + 1) * SLOT, :]
        out_ref[i, SLOT:, :] = flat


def combine(parts):
    top = functools.reduce(jnp.maximum, [p[0] for p in parts])
    weights = [p[1] * jnp.exp(p[0] - top) for p in parts]
    total = sum(weights[1:], weights[0])
    total = jnp.where(total > 0.0, total, 1.0)
    shares = [w / total for w in weights]
    delta = functools.reduce(jnp.add, [w * p[2] for w, p in zip(shares, parts)])
    return shares, top + jnp.log(total), delta


def grads_kernel(scale, idx_ref, cnt_ref, qg_ref, kv_ref, st_ref, out_ref, qg_pad, kv_pad):
    nz, cap, hd = kv_ref.shape[0], qg_ref.shape[1], qg_ref.shape[2] // 2
    qg = padded(qg_pad, qg_ref, 0, 2 * hd)
    kv = padded(kv_pad, kv_ref, 0, 2 * hd)
    q, g, k, v = qg[:, :hd], qg[:, hd:], kv[:, :hd], kv[:, hd:]
    own, flat = [], []
    for i in range(NY):
        c = st_ref[i, :SLOT, 2 * hd :].astype(F32)
        own.append((c[:, 0:1], c[:, 1:2] + c[:, 2:3], c[:, 3:4] + c[:, 4:5]))
        r = st_ref[i, SLOT:, :].astype(F32)
        flat.append((r[0:1], r[1:2] + r[2:3], r[3:4] + r[4:5]))
    shares, _, own_delta = combine(own)
    grad_q = jnp.zeros((SLOT, hd), F32)
    for i in range(NY):
        a = st_ref[i, :SLOT, :hd].astype(F32)
        b = st_ref[i, :SLOT, hd : 2 * hd].astype(F32)
        grad_q = grad_q + shares[i] * (a + (own[i][2] - own_delta) * b)
    _, log_total, delta = combine(flat)
    order_q, order_k = orders(idx_ref, cnt_ref, nz, 1)
    allowed = order_k <= order_q
    s = mm(k, q, NT) * scale
    p = jnp.where(allowed, jnp.exp(jnp.where(allowed, s - log_total, NEG)), 0.0)
    ds = (p * (mm(v, g, NT) - delta)).astype(BF)
    grad_k = (mm(ds, q) * scale).astype(BF).reshape(nz, SLOT, hd)
    grad_v = mm(p.astype(BF), g).astype(BF).reshape(nz, SLOT, hd)
    grad_q = grad_q.astype(BF)
    for i in range(nz):
        out_ref[i, :, :hd] = grad_k[i, :cap]
        out_ref[i, :, hd : 2 * hd] = grad_v[i, :cap]
        out_ref[i, :, 2 * hd :] = grad_q[:cap]


def rows_kernel(
    idx_ref, cnt_ref, z_ref, kv_ref, wq_ref, wk_ref, wv_ref, g_ref, w_ref, x_pad, q_pad
):
    nz, cap, hd = z_ref.shape[0], z_ref.shape[1], wq_ref.shape[1]
    heads, _, cols = g_ref.shape
    k = v = jnp.zeros((cap, hd), F32)
    for i in range(nz):
        k = k + z_ref[i, :, :hd].astype(F32)
        v = v + z_ref[i, :, hd : 2 * hd].astype(F32)
    k, v = k.astype(BF), v.astype(BF)
    q = z_ref[idx_ref[0], :, 2 * hd :]
    for c in range(heads):
        part = pl.ds(c * cols, cols)
        g = mm(q, wq_ref[part, :], NT) + mm(k, wk_ref[part, :], NT) + mm(v, wv_ref[part, :], NT)
        g_ref[c] = g.astype(BF)
    x = padded(x_pad, kv_ref, 2 * hd, kv_ref.shape[2])
    grad_q = padded(q_pad, z_ref, 2 * hd, 3 * hd)
    w = mm(x, grad_q, TN)
    w_ref[...] = w.reshape(w_ref.shape).astype(BF)


def finish_kernel(cnt_ref, idx_ref, sel_ref, g_ref, w_ref, h_out, w_out):
    heads, cap, cols = g_ref.shape
    toks = h_out.shape[0]
    block = idx_ref[0] * NY + idx_ref[1]
    acc = jnp.zeros((toks, cols), F32)
    row = lax.broadcasted_iota(jnp.int32, (toks, cap), 0)
    lane = lax.broadcasted_iota(jnp.int32, (toks, cap), 1)
    for h in range(heads):
        hit = (row == sel_ref[h : h + 1, :cap]) & (lane < cnt_ref[h, block])
        acc = acc + mm(jnp.where(hit, 1.0, 0.0).astype(BF), g_ref[h])
    h_out[...] = acc.astype(BF)
    w = w_ref[...].astype(F32)
    w_out[...] = jnp.sum(w, axis=0)


def body(hidden, upstream, w_query, w_key, w_value, w_output, selected, select_count):
    nz, heads = lax.axis_size("z"), lax.axis_size("head")
    z, y, h = lax.axis_index("z"), lax.axis_index("y"), lax.axis_index("head")
    idx = jnp.stack([z, y, h]).astype(jnp.int32)
    toks, cols = hidden.shape
    hd = w_query.shape[2]
    cap = selected.shape[1] // (nz * NY)
    scale = hd ** (-0.5)
    sel = lax.dynamic_slice_in_dim(selected, (z * NY + y) * cap, cap, 1)
    rest = jnp.full((heads, 128 - 2 * cap), -1, jnp.int32)
    sel = jnp.concatenate([sel, sel + toks, rest], axis=1)
    wq, wk, wv, wo = w_query[0], w_key[0], w_value[0], w_output[0]
    count = select_count
    sds = jax.ShapeDtypeStruct

    def swap(x, axis):
        return lax.all_to_all(x, axis, split_axis=0, concat_axis=0, tiled=True)

    picked = call(
        pick_kernel, sds((heads, 2 * cap, cols), BF), (sel, hidden, upstream), [VMEM] * 3
    )
    rows = swap(picked, "head")
    piece = heads * cols // nz
    to_y, to_z = call(
        project_kernel,
        (sds((NY, cap, 2 * hd), BF), sds((nz, cap, 2 * hd + piece), BF)),
        (idx, count, rows, wq, wk, wv, wo),
        [SMEM] * 2 + [VMEM] * 5,
        [pltpu.VMEM((2 * cap, hd), F32)],
    )
    qg, kv = swap(to_y, "y"), swap(to_z, "z")
    pads = [pltpu.VMEM((NY, SLOT, 2 * hd), BF), pltpu.VMEM((nz, SLOT, 2 * hd), BF)]
    part = call(
        functools.partial(partial_kernel, scale),
        sds((NY, SLOT + 16, 3 * hd), BF),
        (idx, count, qg, kv),
        [SMEM] * 2 + [VMEM] * 2,
        pads,
    )
    joined = swap(part, "y")
    grads = call(
        functools.partial(grads_kernel, scale),
        sds((nz, cap, 3 * hd), BF),
        (idx, count, qg, kv, joined),
        [SMEM] * 2 + [VMEM] * 3,
        pads,
    )
    back = swap(grads, "z")
    grad_rows, weight_terms = call(
        rows_kernel,
        (sds((heads, cap, cols), BF), sds((NY, piece // NY, hd), BF)),
        (idx, count, back, kv, wq, wk, wv),
        [SMEM] * 2 + [VMEM] * 5,
        [pltpu.VMEM((nz, SLOT, piece), BF), pltpu.VMEM((nz, SLOT, hd), BF)],
    )
    returned, terms = swap(grad_rows, "head"), swap(weight_terms, "y")
    grad_hidden, grad_query = call(
        finish_kernel,
        (sds((toks, cols), BF), sds((piece // NY, hd), F32)),
        (count, idx, sel, returned, terms),
        [SMEM] * 2 + [VMEM] * 3,
    )
    return grad_hidden, grad_query[None]


def solution(mesh):
    seq, heads = mesh.devices.shape
    fine = Mesh(mesh.devices.reshape(seq // NY, NY, heads), ("z", "y", "head"))
    both = ("z", "y")
    weight = P("head", None, None)
    in_specs = (P(both, "head"), P(both, "head"), weight, weight, weight, weight, P(), P())
    out_specs = (P(both, "head"), P("head", both, None))
    return jax.shard_map(body, mesh=fine, in_specs=in_specs, out_specs=out_specs, check_vma=False)
```

```python
import functools

import jax
import jax.numpy as jnp
from jax import lax
from jax.experimental import pallas as pl
from jax.experimental.pallas import tpu as pltpu
from jax.sharding import Mesh, PartitionSpec as P

NY = 8
SLOT = 48
WIDE = 256
NEG = -1e30
BF = jnp.bfloat16
F32 = jnp.float32
VMEM = pl.BlockSpec(memory_space=pltpu.VMEM)
SMEM = pl.BlockSpec(memory_space=pltpu.SMEM)
HBM = pl.BlockSpec(memory_space=pl.ANY)
NN = (((1,), (0,)), ((), ()))
NT = (((1,), (1,)), ((), ()))
TN = (((0,), (0,)), ((), ()))


def mm(a, b, dims=NN):
    return lax.dot_general(a, b, dims, preferred_element_type=F32)


def call(kernel, outs, args, specs, scratch=(), limit=16):
    return pl.pallas_call(
        kernel,
        out_shape=outs,
        in_specs=specs,
        out_specs=jax.tree.map(lambda _: VMEM, outs),
        scratch_shapes=list(scratch),
        compiler_params=pltpu.CompilerParams(vmem_limit_bytes=limit << 20),
    )(*args)


def pick_kernel(idx_ref, sel_ref, hid_ref, up_ref, out_ref, mine_ref, table, sems):
    heads, rows, cols = out_ref.shape
    cap, toks = rows // 2, hid_ref.shape[0]
    part = toks // 3
    copies = []
    for i, src in enumerate((hid_ref, up_ref)):
        for j in range(3):
            at = pl.ds(j * part, part)
            dst = table.at[pl.ds(i * toks + j * part, part)]
            copies.append(pltpu.make_async_copy(src.at[at], dst, sems.at[3 * i + j]))
    for copy in copies:
        copy.start()
    start = (idx_ref[0] * NY + idx_ref[1]) * cap
    aligned = jnp.minimum(start // 128 * 128, sel_ref.shape[1] - WIDE)
    window = sel_ref[:, pl.ds(pl.multiple_of(aligned, 128), WIDE)]
    shift = lax.rem(WIDE - (start - aligned), WIDE)
    low = pltpu.roll(window, shift, 1)[:, :128]
    high = pltpu.roll(low, cap, 1) + toks
    lane = lax.broadcasted_iota(jnp.int32, (heads, 128), 1)
    mine = jnp.where(lane < cap, low, high)
    mine_ref[...] = mine
    sel_t = mine.astype(F32).T
    target = jnp.concatenate([sel_t[:rows, h : h + 1] for h in range(heads)], axis=0)
    target = target.astype(jnp.int32)
    lane = lax.broadcasted_iota(jnp.int32, (heads * rows, 2 * toks), 1)
    onehot = jnp.where(lane == target, 1.0, 0.0).astype(BF)
    for copy in copies:
        copy.wait()
    out_ref[...] = mm(onehot, table[...]).reshape(heads, rows, cols).astype(BF)


def pack_kernel(wq_ref, wk_ref, wv_ref, wo_ref, w_ref):
    hd = wq_ref.shape[1]
    w_ref[:, :hd] = wq_ref[...]
    w_ref[:, hd : 2 * hd] = wk_ref[...]
    w_ref[:, 2 * hd : 3 * hd] = wv_ref[...]
    w_ref[:, 3 * hd :] = wo_ref[...].T


def project_kernel(idx_ref, cnt_ref, r_ref, w_ref, z_ref, y_ref, acc):
    heads, rows, cols = r_ref.shape
    cap, hd = rows // 2, w_ref.shape[1] // 4
    total = jnp.zeros((rows, 4 * hd), F32)
    for c in range(heads):
        total = total + mm(r_ref[c], w_ref[pl.ds(c * cols, cols), :])
    acc[...] = total[:, 3 * hd :]
    g = acc[cap:, :]
    count = cnt_ref[idx_ref[2], idx_ref[0] * NY + idx_ref[1]]
    row = lax.broadcasted_iota(jnp.int32, (cap, hd), 0)
    g = jnp.where(row < count, g, 0.0).astype(BF)
    qkv = total[:SLOT, : 3 * hd].astype(BF)[:cap]
    nz = z_ref.shape[0]
    for i in range(nz):
        z_ref[i, :, :hd] = qkv[:, :hd]
        z_ref[i, :, hd:] = g
    wide = heads * cols // (nz * NY)
    for i in range(NY):
        y_ref[i, :, : 2 * hd] = qkv[:, hd:]
        chunks = []
        for j in range(nz):
            c, off = divmod((j * NY + i) * wide, cols)
            base = off // 128 * 128
            aligned = r_ref[c, :, base : base + 128]
            chunks.append(aligned[:cap, off - base : off - base + wide])
        y_ref[i, :, 2 * hd :] = jnp.concatenate(chunks, axis=1)


def padded(pad_ref, ref, lo, hi):
    n, cap = ref.shape[0], ref.shape[1]
    w = hi - lo
    pad_ref[:, SLOT - 16 :, :] = jnp.zeros((n, 16, w), BF)
    for i in range(n):
        pad_ref[i, :cap, :] = ref[i, :, lo:hi]
    return pad_ref[...].reshape(n * SLOT, w)


def orders(idx_ref, cnt_ref, nz, axis_q):
    z, y, h = idx_ref[0], idx_ref[1], idx_ref[2]

    def one(n, axis, block_of, dead):
        shape = (n * SLOT, 1) if axis == 0 else (1, n * SLOT)
        at = lax.broadcasted_iota(jnp.int32, shape, axis)
        out = jnp.full(shape, dead, jnp.int32)
        for i in range(n):
            b = block_of(i)
            c = at - i * SLOT
            live = (c >= 0) & (c < cnt_ref[h, b])
            out = jnp.where(live, c + b * SLOT, out)
        return out

    order_q = one(nz, axis_q, lambda i: i * NY + y, -1)
    order_k = one(NY, 1 - axis_q, lambda i: z * NY + i, 1 << 30)
    return order_q, order_k


def split(x):
    hi = x.astype(BF).astype(F32)
    return hi, x - hi


def partial_kernel(scale, idx_ref, cnt_ref, qg_ref, kv_ref, out_ref, qg_pad, kv_pad):
    nz, cap, hd = qg_ref.shape[0], qg_ref.shape[1], qg_ref.shape[2] // 2
    qg = padded(qg_pad, qg_ref, 0, 2 * hd)
    kv = padded(kv_pad, kv_ref, 0, 2 * hd)
    q, g, k, v = qg[:, :hd], qg[:, hd:], kv[:, :hd], kv[:, hd:]
    order_q, order_k = orders(idx_ref, cnt_ref, nz, 0)
    allowed = order_k <= order_q
    s = jnp.where(allowed, mm(q, k, NT) * scale, NEG)
    top = jnp.max(s, axis=1, keepdims=True)
    e = jnp.where(allowed, jnp.exp(s - top), 0.0)
    total = jnp.sum(e, axis=1, keepdims=True)
    total = jnp.where(total > 0.0, total, 1.0)
    p = e * (1.0 / total)
    gp = mm(g, v, NT)
    delta = jnp.sum(p * gp, axis=1, keepdims=True)
    a = mm((p * (gp - delta)).astype(BF), k) * scale
    b = mm(p.astype(BF), k) * scale
    own = jnp.concatenate([a, b], axis=1).astype(BF)
    n = nz * SLOT
    lane = lax.broadcasted_iota(jnp.int32, (n, 128), 1) % 4
    stats = jnp.zeros((n, 128), F32)
    for i, col in enumerate(split(top + jnp.log(total)) + split(delta)):
        stats = jnp.where(lane == i, col, stats)
    whole = -(-n // WIDE) * WIDE
    if whole > n:
        stats = jnp.concatenate([stats, jnp.zeros((whole - n, 128), F32)], axis=0)
    stats = stats.T[:16, :]
    row = lax.broadcasted_iota(jnp.int32, (16, WIDE), 0) // 4
    flat = jnp.zeros((16, WIDE), F32)
    for j in range(whole // WIDE):
        flat = jnp.where(row == j, stats[:, j * WIDE : (j + 1) * WIDE], flat)
    flat = flat.astype(BF)
    for i in range(nz):
        out_ref[i, :16, :] = flat
        out_ref[i, 16:, :] = own[i * SLOT : (i + 1) * SLOT, :][:cap]


def grads_kernel(
    scale, idx_ref, cnt_ref, qg_ref, kv_ref, st_ref, out_ref, qg_pad, kv_pad, turn
):
    nz, cap, hd = qg_ref.shape[0], qg_ref.shape[1], qg_ref.shape[2] // 2
    n = nz * SLOT
    qg = padded(qg_pad, qg_ref, 0, 2 * hd)
    kv = padded(kv_pad, kv_ref, 0, 2 * hd)
    q, g, k, v = qg[:, :hd], qg[:, hd:], kv[:, :hd], kv[:, hd:]
    chunks = -(-n // WIDE)
    logs, deltas = [], []
    for i in range(nz):
        r = st_ref[i, :16, :].astype(F32)
        line = [jnp.concatenate([r[4 * j + s : 4 * j + s + 1] for j in range(chunks)], axis=1) for s in range(4)]
        logs.append(line[0] + line[1])
        deltas.append(line[2] + line[3])
    top = functools.reduce(jnp.maximum, logs)
    weights = [jnp.exp(x - top) for x in logs]
    total = functools.reduce(jnp.add, weights)
    shares = [w / total for w in weights]
    delta = functools.reduce(jnp.add, [w * d for w, d in zip(shares, deltas)])
    log_total = (top + jnp.log(total))[:, :n]
    width = chunks * WIDE
    lines = shares + [d - delta for d in deltas] + [jnp.zeros((128 - 2 * nz, width), F32)]
    turn[...] = jnp.concatenate(lines, axis=0).T
    delta = delta[:, :n]
    mine = turn[pl.ds(pl.multiple_of(idx_ref[0] * SLOT, SLOT), SLOT), :]
    grad_q = jnp.zeros((cap, hd), F32)
    for i in range(nz):
        a = st_ref[i, 16:, :hd].astype(F32)
        b = st_ref[i, 16:, hd:].astype(F32)
        grad_q = grad_q + mine[:cap, i : i + 1] * (a + mine[:cap, nz + i : nz + i + 1] * b)
    order_q, order_k = orders(idx_ref, cnt_ref, nz, 1)
    allowed = order_k <= order_q
    s = mm(k, q, NT) * scale
    p = jnp.where(allowed, jnp.exp(jnp.where(allowed, s - log_total, NEG)), 0.0)
    ds = (p * (mm(v, g, NT) - delta)).astype(BF)
    grad_k = (mm(ds, q) * scale).astype(BF).reshape(NY, SLOT, hd)
    grad_v = mm(p.astype(BF), g).astype(BF).reshape(NY, SLOT, hd)
    grad_q = grad_q.astype(BF)
    for i in range(NY):
        out_ref[i, :, :hd] = grad_k[i, :cap]
        out_ref[i, :, hd : 2 * hd] = grad_v[i, :cap]
        out_ref[i, :, 2 * hd :] = grad_q


def rows_kernel(idx_ref, back_ref, kv_ref, w_ref, g_ref, t_ref, x_pad, q_pad):
    heads, cap, cols = g_ref.shape
    hd = w_ref.shape[1] // 4
    kv = jnp.zeros((cap, 2 * hd), F32)
    for i in range(NY):
        kv = kv + back_ref[i, :, : 2 * hd].astype(F32)
    qkv = jnp.concatenate([back_ref[idx_ref[1], :, 2 * hd :], kv.astype(BF)], axis=1)
    x = padded(x_pad, kv_ref, 2 * hd, kv_ref.shape[2])
    grad_q = padded(q_pad, back_ref, 2 * hd, 3 * hd)
    t_ref[...] = mm(x, grad_q, TN).reshape(t_ref.shape).astype(BF)
    for c in range(heads):
        g_ref[c] = mm(qkv, w_ref[pl.ds(c * cols, cols), : 3 * hd], NT).astype(BF)


def finish_kernel(idx_ref, cnt_ref, sel_ref, g_ref, t_ref, h_out, w_out):
    heads, cap, cols = g_ref.shape
    toks = h_out.shape[0]
    block = idx_ref[0] * NY + idx_ref[1]
    acc = jnp.zeros((toks, cols), F32)
    row = lax.broadcasted_iota(jnp.int32, (toks, cap), 0)
    lane = lax.broadcasted_iota(jnp.int32, (toks, cap), 1)
    for h in range(heads):
        hit = (row == sel_ref[h : h + 1, :cap]) & (lane < cnt_ref[h, block])
        acc = acc + mm(jnp.where(hit, 1.0, 0.0).astype(BF), g_ref[h])
    h_out[...] = acc.astype(BF)
    w_out[...] = jnp.sum(t_ref[...].astype(F32), axis=0)


def body(hidden, upstream, w_query, w_key, w_value, w_output, selected, select_count):
    nz, heads = lax.axis_size("z"), lax.axis_size("head")
    idx = jnp.stack([lax.axis_index(a) for a in ("z", "y", "head")]).astype(jnp.int32)
    toks, cols = hidden.shape
    hd = w_query.shape[2]
    cap = selected.shape[1] // (nz * NY)
    scale = hd ** (-0.5)
    count = select_count
    sds = jax.ShapeDtypeStruct

    def swap(x, axis):
        return lax.all_to_all(x, axis, split_axis=0, concat_axis=0, tiled=True)

    picked, mine = call(
        pick_kernel,
        (sds((heads, 2 * cap, cols), BF), sds((heads, 128), jnp.int32)),
        (idx, selected, hidden, upstream),
        [SMEM, VMEM, HBM, HBM],
        [pltpu.VMEM((2 * toks, cols), BF), pltpu.SemaphoreType.DMA((6,))],
    )
    rows = swap(picked, "head")
    tall = pl.BlockSpec((cols, hd), lambda i: (i, 0))
    weights = pl.pallas_call(
        pack_kernel,
        grid=(heads,),
        out_shape=sds((heads * cols, 4 * hd), BF),
        in_specs=[tall, tall, tall, pl.BlockSpec((hd, cols), lambda i: (0, i))],
        out_specs=pl.BlockSpec((cols, 4 * hd), lambda i: (i, 0)),
        compiler_params=pltpu.CompilerParams(vmem_limit_bytes=8 << 20),
        cost_estimate=pl.CostEstimate(
            flops=0, bytes_accessed=16 * heads * cols * hd, transcendentals=0
        ),
    )(w_query[0], w_key[0], w_value[0], w_output[0])
    piece = heads * cols // NY
    to_z, to_y = call(
        project_kernel,
        (sds((nz, cap, 2 * hd), BF), sds((NY, cap, 2 * hd + piece), BF)),
        (idx, count, rows, weights),
        [SMEM] * 2 + [VMEM] * 2,
        [pltpu.VMEM((2 * cap, hd), F32)],
    )
    qg, kv = swap(to_z, "z"), swap(to_y, "y")
    pads = [pltpu.VMEM((nz, SLOT, 2 * hd), BF), pltpu.VMEM((NY, SLOT, 2 * hd), BF)]
    part = call(
        functools.partial(partial_kernel, scale),
        sds((nz, cap + 16, 2 * hd), BF),
        (idx, count, qg, kv),
        [SMEM] * 2 + [VMEM] * 2,
        pads,
    )
    joined = swap(part, "z")
    grads = call(
        functools.partial(grads_kernel, scale),
        sds((NY, cap, 3 * hd), BF),
        (idx, count, qg, kv, joined),
        [SMEM] * 2 + [VMEM] * 3,
        pads + [pltpu.VMEM((-(-nz * SLOT // WIDE) * WIDE, 128), F32)],
    )
    back = swap(grads, "y")
    grad_rows, weight_terms = call(
        rows_kernel,
        (sds((heads, cap, cols), BF), sds((nz, piece // nz, hd), BF)),
        (idx, back, kv, weights),
        [SMEM] + [VMEM] * 3,
        [pltpu.VMEM((NY, SLOT, piece), BF), pltpu.VMEM((NY, SLOT, hd), BF)],
    )
    returned, terms = swap(grad_rows, "head"), swap(weight_terms, "z")
    grad_hidden, grad_query = call(
        finish_kernel,
        (sds((toks, cols), BF), sds((piece // nz, hd), F32)),
        (idx, count, mine, returned, terms),
        [SMEM] * 2 + [VMEM] * 3,
    )
    return grad_hidden, grad_query[None]


def solution(mesh):
    seq, heads = mesh.devices.shape
    fine = Mesh(mesh.devices.reshape(seq // NY, NY, heads), ("z", "y", "head"))
    both = ("z", "y")
    weight = P("head", None, None)
    in_specs = (P(both, "head"), P(both, "head"), weight, weight, weight, weight, P(), P())
    out_specs = (P(both, "head"), P("head", both, None))
    return jax.shard_map(body, mesh=fine, in_specs=in_specs, out_specs=out_specs, check_vma=False)
```

```python
import functools

import jax
import jax.numpy as jnp
from jax import lax
from jax.experimental import pallas as pl
from jax.experimental.pallas import tpu as pltpu
from jax.sharding import Mesh, PartitionSpec as P

NY = 8
SLOT = 48
WIDE = 256
NEG = -1e30
BF = jnp.bfloat16
F32 = jnp.float32
VMEM = pl.BlockSpec(memory_space=pltpu.VMEM)
SMEM = pl.BlockSpec(memory_space=pltpu.SMEM)
HBM = pl.BlockSpec(memory_space=pltpu.HBM)
NN = (((1,), (0,)), ((), ()))
NT = (((1,), (1,)), ((), ()))
TN = (((0,), (0,)), ((), ()))


def mm(a, b, dims=NN):
    return lax.dot_general(a, b, dims, preferred_element_type=F32)


def call(kernel, outs, args, specs, scratch=(), limit=16, out_specs=None, cost=None):
    return pl.pallas_call(
        kernel,
        out_shape=outs,
        in_specs=specs,
        out_specs=out_specs or jax.tree.map(lambda _: VMEM, outs),
        scratch_shapes=list(scratch),
        compiler_params=pltpu.CompilerParams(vmem_limit_bytes=limit << 20),
        cost_estimate=cost
        and pl.CostEstimate(flops=cost[0], bytes_accessed=cost[1], transcendentals=0),
    )(*args)


def pick_kernel(
    idx_ref, sel_ref, hid_ref, up_ref, out_ref, mine_ref, table, ready, view, sems, out_sems
):
    heads, rows, cols = out_ref.shape
    cap, toks = rows // 2, hid_ref.shape[0]
    start = (idx_ref[0] * NY + idx_ref[1]) * cap
    aligned = jnp.minimum(start // 128 * 128, sel_ref.shape[1] - WIDE)
    window = pltpu.make_async_copy(
        sel_ref.at[:, pl.ds(pl.multiple_of(aligned, 128), WIDE)], view, sems.at[0]
    )
    window.start()
    part = toks // 3
    copies = []
    for i, src in enumerate((hid_ref, up_ref)):
        for j in range(3):
            dst = table.at[pl.ds(i * toks + j * part, part)]
            copies.append(
                pltpu.make_async_copy(src.at[pl.ds(j * part, part)], dst, sems.at[3 * i + j + 1])
            )
    for copy in copies:
        copy.start()
    window.wait()
    shift = lax.rem(WIDE - (start - aligned), WIDE)
    low = pltpu.roll(view[...], shift, 1)[:, :128]
    high = pltpu.roll(low, cap, 1) + toks
    lane = lax.broadcasted_iota(jnp.int32, (heads, 128), 1)
    mine = jnp.where(lane < cap, low, high)
    mine_ref[...] = mine
    sel_t = mine.astype(F32).T
    target = jnp.concatenate([sel_t[:rows, h : h + 1] for h in range(heads)], axis=0)
    target = target.astype(jnp.int32)
    lane = lax.broadcasted_iota(jnp.int32, (heads * rows, 2 * toks), 1)
    onehot = jnp.where(lane == target, 1.0, 0.0).astype(BF)
    for copy in copies:
        copy.wait()
    some = heads // 2
    outs = []
    for i in range(2):
        got = mm(onehot[i * some * rows : (i + 1) * some * rows], table[...])
        at = pl.ds(i * some, some)
        ready[at] = got.reshape(some, rows, cols).astype(BF)
        outs.append(pltpu.make_async_copy(ready.at[at], out_ref.at[at], out_sems.at[i]))
        outs[i].start()
    for copy in outs:
        copy.wait()


def project_kernel(
    idx_ref,
    cnt_ref,
    r_hbm,
    wq_ref,
    wk_ref,
    wv_ref,
    wo_ref,
    z_ref,
    y_hbm,
    acc,
    r_ref,
    w_in,
    w_up,
    y_ref,
    r_sems,
    w_sems,
    y_sems,
):
    heads, rows, cols = r_ref.shape
    cap, hd = rows // 2, wq_ref.shape[1]
    arrive, loads = [], []
    for c in range(heads):
        arrive.append(pltpu.make_async_copy(r_hbm.at[c], r_ref.at[c], r_sems.at[c]))
        part = pl.ds(c * cols, cols)
        for j, src in enumerate((wq_ref, wk_ref, wv_ref)):
            dst = w_in.at[part, pl.ds(j * hd, hd)]
            loads.append(pltpu.make_async_copy(src.at[part], dst, w_sems.at[c, j]))
        loads.append(pltpu.make_async_copy(wo_ref.at[:, part], w_up.at[:, part], w_sems.at[c, 3]))
    for copy in arrive + loads:
        copy.start()
    for copy in arrive:
        copy.wait()
    nz = cnt_ref.shape[1] // NY
    wide = heads * cols // (nz * NY)
    for i in range(NY):
        chunks = []
        for j in range(nz):
            c, off = divmod((j * NY + i) * wide, cols)
            base = off // 128 * 128
            aligned = r_ref[c, :, base : base + 128]
            chunks.append(aligned[:cap, off - base : off - base + wide])
        y_ref[i, :, 2 * hd :] = jnp.concatenate(chunks, axis=1)
    qkv = jnp.zeros((SLOT, 3 * hd), F32)
    g = jnp.zeros((rows, hd), F32)
    for c in range(heads):
        part = pl.ds(c * cols, cols)
        x = r_ref[c]
        for load in loads[4 * c : 4 * c + 4]:
            load.wait()
        qkv = qkv + mm(x[:SLOT], w_in[part, :])
        g = g + mm(x, w_up[:, part], NT)
    acc[...] = g
    g = acc[cap:, :]
    count = cnt_ref[idx_ref[2], idx_ref[0] * NY + idx_ref[1]]
    row = lax.broadcasted_iota(jnp.int32, (cap, hd), 0)
    g = jnp.where(row < count, g, 0.0).astype(BF)
    qkv = qkv.astype(BF)[:cap]
    leave = []
    for i in range(NY):
        y_ref[i, :, : 2 * hd] = qkv[:, hd:]
        leave.append(pltpu.make_async_copy(y_ref.at[i], y_hbm.at[i], y_sems.at[i]))
        leave[i].start()
    z_ref[0, :, :hd] = qkv[:, :hd]
    z_ref[0, :, hd:] = g
    for copy in leave:
        copy.wait()


def padded(pad_ref, ref, lo, hi):
    n, cap = ref.shape[0], ref.shape[1]
    w = hi - lo
    pad_ref[:, SLOT - 16 :, :] = jnp.zeros((n, 16, w), BF)
    for i in range(n):
        pad_ref[i, :cap, :] = ref[i, :, lo:hi]
    return pad_ref[...].reshape(n * SLOT, w)


def orders(idx_ref, cnt_ref, nz, axis_q):
    z, y, h = idx_ref[0], idx_ref[1], idx_ref[2]

    def one(n, axis, block_of, dead):
        shape = (n * SLOT, 1) if axis == 0 else (1, n * SLOT)
        at = lax.broadcasted_iota(jnp.int32, shape, axis)
        out = jnp.full(shape, dead, jnp.int32)
        for i in range(n):
            b = block_of(i)
            c = at - i * SLOT
            live = (c >= 0) & (c < cnt_ref[h, b])
            out = jnp.where(live, c + b * SLOT, out)
        return out

    order_q = one(nz, axis_q, lambda i: i * NY + y, -1)
    order_k = one(NY, 1 - axis_q, lambda i: z * NY + i, 1 << 30)
    return order_q, order_k


def split(x):
    hi = x.astype(BF).astype(F32)
    return hi, x - hi


def partial_kernel(scale, idx_ref, cnt_ref, qg_ref, kv_ref, out_ref, qg_pad, kv_pad):
    nz, cap, hd = qg_ref.shape[0], qg_ref.shape[1], qg_ref.shape[2] // 2
    qg = padded(qg_pad, qg_ref, 0, 2 * hd)
    kv = padded(kv_pad, kv_ref, 0, 2 * hd)
    q, g, k, v = qg[:, :hd], qg[:, hd:], kv[:, :hd], kv[:, hd:]
    order_q, order_k = orders(idx_ref, cnt_ref, nz, 0)
    allowed = order_k <= order_q
    s = jnp.where(allowed, mm(q, k, NT) * scale, NEG)
    top = jnp.max(s, axis=1, keepdims=True)
    e = jnp.where(allowed, jnp.exp(s - top), 0.0)
    total = jnp.sum(e, axis=1, keepdims=True)
    total = jnp.where(total > 0.0, total, 1.0)
    p = e * (1.0 / total)
    gp = mm(g, v, NT)
    delta = jnp.sum(p * gp, axis=1, keepdims=True)
    a = mm((p * (gp - delta)).astype(BF), k) * scale
    b = mm(p.astype(BF), k) * scale
    own = jnp.concatenate([a, b], axis=1).astype(BF)
    n = nz * SLOT
    lane = lax.broadcasted_iota(jnp.int32, (n, 128), 1) % 4
    stats = jnp.zeros((n, 128), F32)
    for i, col in enumerate(split(top + jnp.log(total)) + split(delta)):
        stats = jnp.where(lane == i, col, stats)
    whole = -(-n // WIDE) * WIDE
    if whole > n:
        stats = jnp.concatenate([stats, jnp.zeros((whole - n, 128), F32)], axis=0)
    stats = stats.T[:16, :]
    row = lax.broadcasted_iota(jnp.int32, (16, WIDE), 0) // 4
    flat = jnp.zeros((16, WIDE), F32)
    for j in range(whole // WIDE):
        flat = jnp.where(row == j, stats[:, j * WIDE : (j + 1) * WIDE], flat)
    flat = flat.astype(BF)
    for i in range(nz):
        out_ref[i, :16, :] = flat
        out_ref[i, 16:, :] = own[i * SLOT : (i + 1) * SLOT, :][:cap]


def grads_kernel(
    scale, idx_ref, cnt_ref, qg_ref, kv_ref, st_ref, out_ref, qg_pad, kv_pad, turn
):
    nz, cap, hd = qg_ref.shape[0], qg_ref.shape[1], qg_ref.shape[2] // 2
    n = nz * SLOT
    qg = padded(qg_pad, qg_ref, 0, 2 * hd)
    kv = padded(kv_pad, kv_ref, 0, 2 * hd)
    q, g, k, v = qg[:, :hd], qg[:, hd:], kv[:, :hd], kv[:, hd:]
    chunks = -(-n // WIDE)
    logs, deltas = [], []
    for i in range(nz):
        r = st_ref[i, :16, :].astype(F32)
        line = [jnp.concatenate([r[4 * j + s : 4 * j + s + 1] for j in range(chunks)], axis=1) for s in range(4)]
        logs.append(line[0] + line[1])
        deltas.append(line[2] + line[3])
    top = functools.reduce(jnp.maximum, logs)
    weights = [jnp.exp(x - top) for x in logs]
    total = functools.reduce(jnp.add, weights)
    shares = [w / total for w in weights]
    delta = functools.reduce(jnp.add, [w * d for w, d in zip(shares, deltas)])
    log_total = (top + jnp.log(total))[:, :n]
    width = chunks * WIDE
    lines = shares + [d - delta for d in deltas] + [jnp.zeros((128 - 2 * nz, width), F32)]
    turn[...] = jnp.concatenate(lines, axis=0).T
    delta = delta[:, :n]
    mine = turn[pl.ds(pl.multiple_of(idx_ref[0] * SLOT, SLOT), SLOT), :]
    grad_q = jnp.zeros((cap, hd), F32)
    for i in range(nz):
        a = st_ref[i, 16:, :hd].astype(F32)
        b = st_ref[i, 16:, hd:].astype(F32)
        grad_q = grad_q + mine[:cap, i : i + 1] * (a + mine[:cap, nz + i : nz + i + 1] * b)
    order_q, order_k = orders(idx_ref, cnt_ref, nz, 1)
    allowed = order_k <= order_q
    s = mm(k, q, NT) * scale
    p = jnp.where(allowed, jnp.exp(jnp.where(allowed, s - log_total, NEG)), 0.0)
    ds = (p * (mm(v, g, NT) - delta)).astype(BF)
    grad_k = (mm(ds, q) * scale).astype(BF).reshape(NY, SLOT, hd)
    grad_v = mm(p.astype(BF), g).astype(BF).reshape(NY, SLOT, hd)
    grad_q = grad_q.astype(BF)
    for i in range(NY):
        out_ref[i, :, :hd] = grad_k[i, :cap]
        out_ref[i, :, hd : 2 * hd] = grad_v[i, :cap]
        out_ref[i, :, 2 * hd :] = grad_q


def rows_kernel(idx_ref, back_ref, wq_ref, wk_ref, wv_ref, g_ref):
    heads, cap, cols = g_ref.shape
    hd = wq_ref.shape[1]
    kv = jnp.zeros((cap, 2 * hd), F32)
    for i in range(NY):
        kv = kv + back_ref[i, :, : 2 * hd].astype(F32)
    qkv = jnp.concatenate([back_ref[idx_ref[1], :, 2 * hd :], kv.astype(BF)], axis=1)
    for c in range(heads):
        part = pl.ds(c * cols, cols)
        w = jnp.concatenate([wq_ref[part, :], wk_ref[part, :], wv_ref[part, :]], axis=1)
        g_ref[c] = mm(qkv, w, NT).astype(BF)


def weight_kernel(back_ref, kv_ref, t_ref, x_pad, q_pad):
    hd = t_ref.shape[2]
    x = padded(x_pad, kv_ref, 2 * hd, kv_ref.shape[2])
    grad_q = padded(q_pad, back_ref, 2 * hd, 3 * hd)
    t_ref[...] = mm(x, grad_q, TN).reshape(t_ref.shape).astype(BF)


def scatter_kernel(idx_ref, cnt_ref, sel_ref, g_ref, h_out):
    heads, cap, cols = g_ref.shape
    toks = h_out.shape[0]
    block = idx_ref[0] * NY + idx_ref[1]
    acc = jnp.zeros((toks, cols), F32)
    row = lax.broadcasted_iota(jnp.int32, (toks, cap), 0)
    lane = lax.broadcasted_iota(jnp.int32, (toks, cap), 1)
    for h in range(heads):
        hit = (row == sel_ref[h : h + 1, :cap]) & (lane < cnt_ref[h, block])
        acc = acc + mm(jnp.where(hit, 1.0, 0.0).astype(BF), g_ref[h])
    h_out[...] = acc.astype(BF)


def body(hidden, upstream, w_query, w_key, w_value, w_output, selected, select_count):
    nz, heads = lax.axis_size("z"), lax.axis_size("head")
    idx = jnp.stack([lax.axis_index(a) for a in ("z", "y", "head")]).astype(jnp.int32)
    toks, cols = hidden.shape
    hd = w_query.shape[2]
    cap = selected.shape[1] // (nz * NY)
    scale = hd ** (-0.5)
    count = select_count
    sds = jax.ShapeDtypeStruct

    def swap(x, axis):
        return lax.all_to_all(x, axis, split_axis=0, concat_axis=0, tiled=True)

    picked, mine = call(
        pick_kernel,
        (sds((heads, 2 * cap, cols), BF), sds((heads, 128), jnp.int32)),
        (idx, selected, hidden, upstream),
        [SMEM, HBM, HBM, HBM],
        [
            pltpu.VMEM((2 * toks, cols), BF),
            pltpu.VMEM((heads, 2 * cap, cols), BF),
            pltpu.VMEM((heads, WIDE), jnp.int32),
            pltpu.SemaphoreType.DMA((7,)),
            pltpu.SemaphoreType.DMA((2,)),
        ],
        limit=60,
        out_specs=(HBM, VMEM),
    )
    rows = swap(picked, "head")
    piece = heads * cols // NY
    to_z, to_y = call(
        project_kernel,
        (sds((1, cap, 2 * hd), BF), sds((NY, cap, 2 * hd + piece), BF)),
        (idx, count, rows, w_query[0], w_key[0], w_value[0], w_output[0]),
        [SMEM] * 2 + [HBM] * 5,
        [
            pltpu.VMEM((2 * cap, hd), F32),
            pltpu.VMEM((heads, 2 * cap, cols), BF),
            pltpu.VMEM((heads * cols, 3 * hd), BF),
            pltpu.VMEM((hd, heads * cols), BF),
            pltpu.VMEM((NY, cap, 2 * hd + piece), BF),
            pltpu.SemaphoreType.DMA((heads,)),
            pltpu.SemaphoreType.DMA((heads, 4)),
            pltpu.SemaphoreType.DMA((NY,)),
        ],
        limit=60,
        out_specs=(VMEM, HBM),
    )
    qg = lax.all_gather(to_z, "z", axis=0, tiled=True)
    kv = swap(to_y, "y")
    pads = [pltpu.VMEM((nz, SLOT, 2 * hd), BF), pltpu.VMEM((NY, SLOT, 2 * hd), BF)]
    part = call(
        functools.partial(partial_kernel, scale),
        sds((nz, cap + 16, 2 * hd), BF),
        (idx, count, qg, kv),
        [SMEM] * 2 + [VMEM] * 2,
        pads,
    )
    joined = swap(part, "z")
    grads = call(
        functools.partial(grads_kernel, scale),
        sds((NY, cap, 3 * hd), BF),
        (idx, count, qg, kv, joined),
        [SMEM] * 2 + [VMEM] * 3,
        pads + [pltpu.VMEM((-(-nz * SLOT // WIDE) * WIDE, 128), F32)],
    )
    back = swap(grads, "y")
    size = heads * cap * cols
    grad_rows = call(
        rows_kernel,
        sds((heads, cap, cols), BF),
        (idx, back, w_query[0], w_key[0], w_value[0]),
        [SMEM] + [VMEM] * 4,
        cost=(6 * hd * size, 8 * size),
    )
    weight_terms = call(
        weight_kernel,
        sds((nz, piece // nz, hd), BF),
        (back, kv),
        [VMEM] * 2,
        [pltpu.VMEM((NY, SLOT, piece), BF), pltpu.VMEM((NY, SLOT, hd), BF)],
        cost=(2 * NY * SLOT * piece * hd, 4 * NY * SLOT * piece),
    )
    returned = swap(grad_rows, "head")
    returned, weight_terms = lax.optimization_barrier((returned, weight_terms))
    terms = swap(weight_terms, "z")
    grad_hidden = call(
        scatter_kernel,
        sds((toks, cols), BF),
        (idx, count, mine, returned),
        [SMEM] * 2 + [VMEM] * 2,
        cost=(2 * toks * size, 4 * size),
    )
    grad_query = jnp.sum(terms.astype(F32), axis=0)
    return grad_hidden, grad_query[None]


def solution(mesh):
    seq, heads = mesh.devices.shape
    fine = Mesh(mesh.devices.reshape(seq // NY, NY, heads), ("z", "y", "head"))
    both = ("z", "y")
    weight = P("head", None, None)
    in_specs = (P(both, "head"), P(both, "head"), weight, weight, weight, weight, P(), P())
    out_specs = (P(both, "head"), P("head", both, None))
    return jax.shard_map(body, mesh=fine, in_specs=in_specs, out_specs=out_specs, check_vma=False)
```

```python
import functools

import jax
import jax.numpy as jnp
from jax import lax
from jax.experimental import pallas as pl
from jax.experimental.pallas import tpu as pltpu
from jax.sharding import Mesh, PartitionSpec as P

NY = 8
SLOT = 48
WIDE = 256
NEG = -1e30
BF = jnp.bfloat16
F32 = jnp.float32
VMEM = pl.BlockSpec(memory_space=pltpu.VMEM)
SMEM = pl.BlockSpec(memory_space=pltpu.SMEM)
HBM = pl.BlockSpec(memory_space=pltpu.HBM)
NN = (((1,), (0,)), ((), ()))
NT = (((1,), (1,)), ((), ()))
TN = (((0,), (0,)), ((), ()))


def mm(a, b, dims=NN):
    return lax.dot_general(a, b, dims, preferred_element_type=F32)


def call(kernel, outs, args, specs, scratch=(), limit=16, out_specs=None):
    return pl.pallas_call(
        kernel,
        out_shape=outs,
        in_specs=specs,
        out_specs=out_specs or jax.tree.map(lambda _: VMEM, outs),
        scratch_shapes=list(scratch),
        compiler_params=pltpu.CompilerParams(vmem_limit_bytes=limit << 20),
    )(*args)


def pick_kernel(
    sel_ref, hid_ref, up_ref, out_ref, mine_ref, table, ready, view, sems, out_sems
):
    heads, rows, cols = out_ref.shape
    cap, toks = rows // 2, hid_ref.shape[0]
    start = (lax.axis_index("z") * NY + lax.axis_index("y")) * cap
    aligned = jnp.minimum(start // 128 * 128, sel_ref.shape[1] - WIDE)
    window = pltpu.make_async_copy(
        sel_ref.at[:, pl.ds(pl.multiple_of(aligned, 128), WIDE)], view, sems.at[0]
    )
    window.start()
    part = toks // 3
    copies = []
    for i, src in enumerate((hid_ref, up_ref)):
        for j in range(3):
            dst = table.at[pl.ds(i * toks + j * part, part)]
            copies.append(
                pltpu.make_async_copy(src.at[pl.ds(j * part, part)], dst, sems.at[3 * i + j + 1])
            )
    for copy in copies:
        copy.start()
    window.wait()
    shift = lax.rem(WIDE - (start - aligned), WIDE)
    low = pltpu.roll(view[...], shift, 1)[:, :128]
    high = pltpu.roll(low, cap, 1) + toks
    lane = lax.broadcasted_iota(jnp.int32, (heads, 128), 1)
    mine = jnp.where(lane < cap, low, high)
    mine_ref[...] = mine
    sel_t = mine.astype(F32).T
    target = jnp.concatenate([sel_t[:rows, h : h + 1] for h in range(heads)], axis=0)
    target = target.astype(jnp.int32)
    lane = lax.broadcasted_iota(jnp.int32, (heads * rows, 2 * toks), 1)
    onehot = jnp.where(lane == target, 1.0, 0.0).astype(BF)
    for copy in copies:
        copy.wait()
    parts = out_sems.shape[0]
    some = heads // parts
    outs = []
    for i in range(parts):
        got = mm(onehot[i * some * rows : (i + 1) * some * rows], table[...])
        at = pl.ds(i * some, some)
        ready[at] = got.reshape(some, rows, cols).astype(BF)
        outs.append(pltpu.make_async_copy(ready.at[at], out_ref.at[at], out_sems.at[i]))
        outs[i].start()
    for copy in outs:
        copy.wait()


def project_kernel(
    live_ref, cnt_ref, r_ref, wq_ref, wk_ref, wv_ref, wo_ref, z_ref, y_hbm, acc, w_in, w_up, y_ref, w_sems, y_sems
):
    heads, rows, cols = r_ref.shape
    cap, hd = rows // 2, wq_ref.shape[1]
    loads = []
    for c in range(heads):
        part = pl.ds(c * cols, cols)
        for j, src in enumerate((wk_ref, wv_ref)):
            dst = w_in.at[j, part]
            loads.append(pltpu.make_async_copy(src.at[part], dst, w_sems.at[c, j]))
        loads.append(pltpu.make_async_copy(wo_ref.at[:, part], w_up.at[:, part], w_sems.at[c, 2]))
    for copy in loads:
        copy.start()
    nz = cnt_ref.shape[1] // NY
    wide = heads * cols // (nz * NY)
    leave = []
    for i in range(NY):
        for at in (pl.ds(2 * hd, nz * wide), pl.ds(0, 2 * hd)):
            sem = y_sems.at[len(leave)]
            leave.append(pltpu.make_async_copy(y_ref.at[i, :, at], y_hbm.at[i, :, at], sem))

    def spread(i):
        chunks = []
        for j in range(nz):
            c, off = divmod((j * NY + i) * wide, cols)
            base = off // 128 * 128
            aligned = r_ref[c, :, base : base + 128]
            chunks.append(aligned[:cap, off - base : off - base + wide])
        y_ref[i, :, 2 * hd :] = jnp.concatenate(chunks, axis=1)
        leave[2 * i].start()

    qkv = jnp.zeros((SLOT, 3 * hd), F32)
    g = jnp.zeros((rows, hd), F32)
    for c in range(heads):
        part = pl.ds(c * cols, cols)
        for i in range(c * NY // heads, (c + 1) * NY // heads):
            spread(i)
        x = r_ref[c]
        for load in loads[3 * c : 3 * c + 3]:
            load.wait()
        w = jnp.concatenate([wq_ref[part, :], w_in[0, part, :], w_in[1, part, :]], axis=1)
        qkv = qkv + mm(x[:SLOT], w)
        g = g + mm(x, w_up[:, part], NT)
    acc[...] = g
    g = acc[cap:, :]
    row = lax.broadcasted_iota(jnp.int32, (cap, hd), 0)
    g = jnp.where(row < live_ref[0, 0], g, 0.0).astype(BF)
    qkv = qkv.astype(BF)[:cap]
    for i in range(NY):
        y_ref[i, :, : 2 * hd] = qkv[:, hd:]
        leave[2 * i + 1].start()
    z_ref[0, :, :hd] = qkv[:, :hd]
    z_ref[0, :, hd:] = g
    for copy in leave:
        copy.wait()


def padded(pad_ref, ref, lo, hi):
    n, cap = ref.shape[0], ref.shape[1]
    w = hi - lo
    pad_ref[:, SLOT - 16 :, :] = jnp.zeros((n, 16, w), BF)
    for i in range(n):
        pad_ref[i, :cap, :] = ref[i, :, lo:hi]
    return pad_ref[...].reshape(n * SLOT, w)


def orders(idx_ref, cnt_ref, nz, axis_q):
    z, y, h = idx_ref[0], idx_ref[1], idx_ref[2]

    def one(n, axis, block_of, dead):
        shape = (n * SLOT, 1) if axis == 0 else (1, n * SLOT)
        at = lax.broadcasted_iota(jnp.int32, shape, axis)
        out = jnp.full(shape, dead, jnp.int32)
        for i in range(n):
            b = block_of(i)
            c = at - i * SLOT
            live = (c >= 0) & (c < cnt_ref[h, b])
            out = jnp.where(live, c + b * SLOT, out)
        return out

    order_q = one(nz, axis_q, lambda i: i * NY + y, -1)
    order_k = one(NY, 1 - axis_q, lambda i: z * NY + i, 1 << 30)
    return order_q, order_k


def split(x):
    hi = x.astype(BF).astype(F32)
    return hi, x - hi


def partial_kernel(scale, idx_ref, cnt_ref, qg_ref, kv_ref, out_ref, qg_pad, kv_pad):
    nz, cap, hd = qg_ref.shape[0], qg_ref.shape[1], qg_ref.shape[2] // 2
    qg = padded(qg_pad, qg_ref, 0, 2 * hd)
    kv = padded(kv_pad, kv_ref, 0, 2 * hd)
    q, g, k, v = qg[:, :hd], qg[:, hd:], kv[:, :hd], kv[:, hd:]
    order_q, order_k = orders(idx_ref, cnt_ref, nz, 0)
    allowed = order_k <= order_q
    s = jnp.where(allowed, mm(q, k, NT) * scale, NEG)
    top = jnp.max(s, axis=1, keepdims=True)
    e = jnp.where(allowed, jnp.exp(s - top), 0.0)
    total = jnp.sum(e, axis=1, keepdims=True)
    total = jnp.where(total > 0.0, total, 1.0)
    p = e * (1.0 / total)
    gp = mm(g, v, NT)
    delta = jnp.sum(p * gp, axis=1, keepdims=True)
    a = mm((p * (gp - delta)).astype(BF), k) * scale
    b = mm(p.astype(BF), k) * scale
    own = jnp.concatenate([a, b], axis=1)
    n = nz * SLOT
    lane = (lax.broadcasted_iota(jnp.int32, (n, 128), 1) - cap) % 4
    stats = jnp.zeros((n, 128), F32)
    for i, col in enumerate(split(top + jnp.log(total)) + split(delta)):
        stats = jnp.where(lane == i, col, stats)
    whole = -(-n // WIDE) * WIDE
    if whole > n:
        stats = jnp.concatenate([stats, jnp.zeros((whole - n, 128), F32)], axis=0)
    stats = stats.T[:SLOT, :]
    row = lax.broadcasted_iota(jnp.int32, (SLOT, WIDE), 0)
    flat = jnp.zeros((SLOT, WIDE), F32)
    for j in range(whole // WIDE):
        flat = jnp.where((row - cap) // 4 == j, stats[:, j * WIDE : (j + 1) * WIDE], flat)
    for i in range(nz):
        out_ref[i] = jnp.where(row < cap, own[i * SLOT : (i + 1) * SLOT, :], flat).astype(BF)


def grads_kernel(
    scale, idx_ref, cnt_ref, qg_ref, kv_ref, st_ref, out_ref, qg_pad, kv_pad, turn
):
    nz, cap, hd = qg_ref.shape[0], qg_ref.shape[1], qg_ref.shape[2] // 2
    n = nz * SLOT
    qg = padded(qg_pad, qg_ref, 0, 2 * hd)
    kv = padded(kv_pad, kv_ref, 0, 2 * hd)
    q, g, k, v = qg[:, :hd], qg[:, hd:], kv[:, :hd], kv[:, hd:]
    chunks = -(-n // WIDE)
    logs, deltas = [], []
    for i in range(nz):
        r = st_ref[i].astype(F32)[cap:]
        line = [jnp.concatenate([r[4 * j + s : 4 * j + s + 1] for j in range(chunks)], axis=1) for s in range(4)]
        logs.append(line[0] + line[1])
        deltas.append(line[2] + line[3])
    top = functools.reduce(jnp.maximum, logs)
    weights = [jnp.exp(x - top) for x in logs]
    total = functools.reduce(jnp.add, weights)
    shares = [w / total for w in weights]
    delta = functools.reduce(jnp.add, [w * d for w, d in zip(shares, deltas)])
    log_total = (top + jnp.log(total))[:, :n]
    width = chunks * WIDE
    lines = shares + [d - delta for d in deltas] + [jnp.zeros((128 - 2 * nz, width), F32)]
    turn[...] = jnp.concatenate(lines, axis=0).T
    delta = delta[:, :n]
    mine = turn[pl.ds(pl.multiple_of(idx_ref[0] * SLOT, SLOT), SLOT), :]
    grad_q = jnp.zeros((cap, hd), F32)
    for i in range(nz):
        a = st_ref[i, :cap, :hd].astype(F32)
        b = st_ref[i, :cap, hd:].astype(F32)
        grad_q = grad_q + mine[:cap, i : i + 1] * (a + mine[:cap, nz + i : nz + i + 1] * b)
    order_q, order_k = orders(idx_ref, cnt_ref, nz, 1)
    allowed = order_k <= order_q
    s = mm(k, q, NT) * scale
    p = jnp.where(allowed, jnp.exp(jnp.where(allowed, s - log_total, NEG)), 0.0)
    ds = (p * (mm(v, g, NT) - delta)).astype(BF)
    grad_k = (mm(ds, q) * scale).astype(BF).reshape(NY, SLOT, hd)
    grad_v = mm(p.astype(BF), g).astype(BF).reshape(NY, SLOT, hd)
    grad_q = grad_q.astype(BF)
    for i in range(NY):
        out_ref[i, :, :hd] = grad_k[i, :cap]
        out_ref[i, :, hd : 2 * hd] = grad_v[i, :cap]
        out_ref[i, :, 2 * hd :] = grad_q


def rows_kernel(idx_ref, back_ref, kv_ref, wq_ref, wk_ref, wv_ref, g_ref, t_ref, x_pad, q_pad):
    heads, cap, cols = g_ref.shape
    hd = wq_ref.shape[1]
    kv = jnp.zeros((cap, 2 * hd), F32)
    for i in range(NY):
        kv = kv + back_ref[i, :, : 2 * hd].astype(F32)
    qkv = jnp.concatenate([back_ref[idx_ref[1], :, 2 * hd :], kv.astype(BF)], axis=1)
    x = padded(x_pad, kv_ref, 2 * hd, kv_ref.shape[2])
    grad_q = padded(q_pad, back_ref, 2 * hd, 3 * hd)
    t_ref[...] = mm(x, grad_q, TN).reshape(t_ref.shape).astype(BF)
    for c in range(heads):
        part = pl.ds(c * cols, cols)
        w = jnp.concatenate([wq_ref[part, :], wk_ref[part, :], wv_ref[part, :]], axis=1)
        g_ref[c] = mm(qkv, w, NT).astype(BF)


def finish_kernel(idx_ref, cnt_ref, sel_ref, g_ref, t_ref, h_out, w_out, pad_ref):
    heads, cap, cols = g_ref.shape
    toks = h_out.shape[0]
    block = idx_ref[0] * NY + idx_ref[1]
    column = sel_ref[...].astype(F32).T
    row = lax.broadcasted_iota(jnp.int32, (SLOT, 1), 0)
    target = []
    for h in range(heads):
        at = column[:SLOT, h : h + 1].astype(jnp.int32)
        target.append(jnp.where(row < cnt_ref[h, block], at, -1))
    target = jnp.concatenate(target, axis=0)
    lane = lax.broadcasted_iota(jnp.int32, (heads * SLOT, toks), 1)
    hit = jnp.where(lane == target, 1.0, 0.0).astype(BF)
    grads = padded(pad_ref, g_ref, 0, cols)
    h_out[...] = mm(hit, grads, TN).astype(BF)
    w_out[...] = jnp.sum(t_ref[...].astype(F32), axis=0)


def body(hidden, upstream, w_query, w_key, w_value, w_output, selected, select_count):
    nz, heads = lax.axis_size("z"), lax.axis_size("head")
    idx = jnp.stack([lax.axis_index(a) for a in ("z", "y", "head")]).astype(jnp.int32)
    toks, cols = hidden.shape
    hd = w_query.shape[2]
    cap = selected.shape[1] // (nz * NY)
    scale = hd ** (-0.5)
    count = select_count
    live = lax.dynamic_slice(select_count, (idx[2], idx[0] * NY + idx[1]), (1, 1))
    sds = jax.ShapeDtypeStruct

    def swap(x, axis):
        return lax.all_to_all(x, axis, split_axis=0, concat_axis=0, tiled=True)

    picked, mine = call(
        pick_kernel,
        (sds((heads, 2 * cap, cols), BF), sds((heads, 128), jnp.int32)),
        (selected, hidden, upstream),
        [HBM, HBM, HBM],
        [
            pltpu.VMEM((2 * toks, cols), BF),
            pltpu.VMEM((heads, 2 * cap, cols), BF),
            pltpu.VMEM((heads, WIDE), jnp.int32),
            pltpu.SemaphoreType.DMA((7,)),
            pltpu.SemaphoreType.DMA((min(heads, 4),)),
        ],
        limit=54,
        out_specs=(HBM, VMEM),
    )
    rows = swap(picked, "head")
    piece = heads * cols // NY
    to_z, to_y = call(
        project_kernel,
        (sds((1, cap, 2 * hd), BF), sds((NY, cap, 2 * hd + piece), BF)),
        (live, count, rows, w_query[0], w_key[0], w_value[0], w_output[0]),
        [SMEM] * 2 + [VMEM] * 2 + [HBM] * 3,
        [
            pltpu.VMEM((2 * cap, hd), F32),
            pltpu.VMEM((2, heads * cols, hd), BF),
            pltpu.VMEM((hd, heads * cols), BF),
            pltpu.VMEM((NY, cap, 2 * hd + piece), BF),
            pltpu.SemaphoreType.DMA((heads, 3)),
            pltpu.SemaphoreType.DMA((2 * NY,)),
        ],
        limit=50,
        out_specs=(VMEM, HBM),
    )
    qg = lax.all_gather(to_z, "z", axis=0, tiled=True)
    kv = swap(to_y, "y")
    pads = [pltpu.VMEM((nz, SLOT, 2 * hd), BF), pltpu.VMEM((NY, SLOT, 2 * hd), BF)]
    part = call(
        functools.partial(partial_kernel, scale),
        sds((nz, SLOT, 2 * hd), BF),
        (idx, count, qg, kv),
        [SMEM] * 2 + [VMEM] * 2,
        pads,
    )
    joined = swap(part, "z")
    grads = call(
        functools.partial(grads_kernel, scale),
        sds((NY, cap, 3 * hd), BF),
        (idx, count, qg, kv, joined),
        [SMEM] * 2 + [VMEM] * 3,
        pads + [pltpu.VMEM((-(-nz * SLOT // WIDE) * WIDE, 128), F32)],
    )
    back = swap(grads, "y")
    grad_rows, weight_terms = call(
        rows_kernel,
        (sds((heads, cap, cols), BF), sds((nz, piece // nz, hd), BF)),
        (idx, back, kv, w_query[0], w_key[0], w_value[0]),
        [SMEM] + [VMEM] * 5,
        [pltpu.VMEM((NY, SLOT, piece), BF), pltpu.VMEM((NY, SLOT, hd), BF)],
    )
    returned, terms = swap(grad_rows, "head"), swap(weight_terms, "z")
    grad_hidden, grad_query = call(
        finish_kernel,
        (sds((toks, cols), BF), sds((piece // nz, hd), F32)),
        (idx, count, mine, returned, terms),
        [SMEM] * 2 + [VMEM] * 3,
        [pltpu.VMEM((heads, SLOT, cols), BF)],
    )
    return grad_hidden, grad_query[None]


def solution(mesh):
    seq, heads = mesh.devices.shape
    fine = Mesh(mesh.devices.reshape(seq // NY, NY, heads), ("z", "y", "head"))
    both = ("z", "y")
    weight = P("head", None, None)
    in_specs = (P(both, "head"), P(both, "head"), weight, weight, weight, weight, P(), P())
    out_specs = (P(both, "head"), P("head", both, None))
    return jax.shard_map(body, mesh=fine, in_specs=in_specs, out_specs=out_specs, check_vma=False)
```

```python
import functools

import jax
import jax.numpy as jnp
from jax import lax
from jax.experimental import pallas as pl
from jax.experimental.pallas import tpu as pltpu
from jax.sharding import Mesh, PartitionSpec as P

NY = 8
SLOT = 48
WIDE = 256
NEG = -1e30
BF = jnp.bfloat16
F32 = jnp.float32
VMEM = pl.BlockSpec(memory_space=pltpu.VMEM)
SMEM = pl.BlockSpec(memory_space=pltpu.SMEM)
HBM = pl.BlockSpec(memory_space=pltpu.HBM)
NN = (((1,), (0,)), ((), ()))
NT = (((1,), (1,)), ((), ()))
TN = (((0,), (0,)), ((), ()))


def mm(a, b, dims=NN):
    return lax.dot_general(a, b, dims, preferred_element_type=F32)


def call(kernel, outs, args, specs, scratch=(), limit=16, out_specs=None):
    return pl.pallas_call(
        kernel,
        out_shape=outs,
        in_specs=specs,
        out_specs=out_specs or jax.tree.map(lambda _: VMEM, outs),
        scratch_shapes=list(scratch),
        compiler_params=pltpu.CompilerParams(vmem_limit_bytes=limit << 20),
    )(*args)


def pick_kernel(
    sel_ref, hid_ref, up_ref, out_ref, mine_ref, table, ready, view, sems, out_sems
):
    heads, rows, cols = out_ref.shape
    cap, toks = rows // 2, hid_ref.shape[0]
    start = (lax.axis_index("z") * NY + lax.axis_index("y")) * cap
    aligned = jnp.minimum(start // 128 * 128, sel_ref.shape[1] - WIDE)
    window = pltpu.make_async_copy(
        sel_ref.at[:, pl.ds(pl.multiple_of(aligned, 128), WIDE)], view, sems.at[0]
    )
    window.start()
    part = toks // 3
    copies = []
    for i, src in enumerate((hid_ref, up_ref)):
        for j in range(3):
            dst = table.at[pl.ds(i * toks + j * part, part)]
            copies.append(
                pltpu.make_async_copy(src.at[pl.ds(j * part, part)], dst, sems.at[3 * i + j + 1])
            )
    for copy in copies:
        copy.start()
    window.wait()
    shift = lax.rem(WIDE - (start - aligned), WIDE)
    low = pltpu.roll(view[...], shift, 1)[:, :128]
    high = pltpu.roll(low, cap, 1) + toks
    lane = lax.broadcasted_iota(jnp.int32, (heads, 128), 1)
    mine = jnp.where(lane < cap, low, high)
    mine_ref[...] = mine
    sel_t = mine.astype(F32).T
    target = jnp.concatenate([sel_t[:rows, h : h + 1] for h in range(heads)], axis=0)
    target = target.astype(jnp.int32)
    lane = lax.broadcasted_iota(jnp.int32, (heads * rows, 2 * toks), 1)
    onehot = jnp.where(lane == target, 1.0, 0.0).astype(BF)
    for copy in copies:
        copy.wait()
    parts = out_sems.shape[0]
    some = heads // parts
    outs = []
    for i in range(parts):
        got = mm(onehot[i * some * rows : (i + 1) * some * rows], table[...])
        at = pl.ds(i * some, some)
        ready[at] = got.reshape(some, rows, cols).astype(BF)
        outs.append(pltpu.make_async_copy(ready.at[at], out_ref.at[at], out_sems.at[i]))
        outs[i].start()
    for copy in outs:
        copy.wait()


def project_kernel(
    nz, block_ref, cnt_ref, r_ref, wq_ref, wk_ref, wv_ref, wo_ref, z_ref, y_hbm, acc, y_ref, counts, y_sems, sem
):
    heads, rows, cols = r_ref.shape
    cap, hd = rows // 2, wq_ref.shape[1]
    number = pltpu.make_async_copy(cnt_ref, counts, sem)
    number.start()
    wide = heads * cols // (nz * NY)
    leave = []
    for i in range(NY):
        for at in (pl.ds(2 * hd, nz * wide), pl.ds(0, 2 * hd)):
            sem = y_sems.at[len(leave)]
            leave.append(pltpu.make_async_copy(y_ref.at[i, :, at], y_hbm.at[i, :, at], sem))

    def spread(i):
        chunks = []
        for j in range(nz):
            c, off = divmod((j * NY + i) * wide, cols)
            base = off // 128 * 128
            aligned = r_ref[c, :, base : base + 128]
            chunks.append(aligned[:cap, off - base : off - base + wide])
        y_ref[i, :, 2 * hd :] = jnp.concatenate(chunks, axis=1)
        leave[2 * i].start()

    qkv = jnp.zeros((SLOT, 3 * hd), F32)
    g = jnp.zeros((rows, hd), F32)
    for c in range(heads):
        part = pl.ds(c * cols, cols)
        for i in range(c * NY // heads, (c + 1) * NY // heads):
            spread(i)
        x = r_ref[c]
        w = jnp.concatenate([wq_ref[part, :], wk_ref[part, :], wv_ref[part, :]], axis=1)
        qkv = qkv + mm(x[:SLOT], w)
        g = g + mm(x, wo_ref[:, part], NT)
    acc[...] = g
    g = acc[cap:, :]
    number.wait()
    row = lax.broadcasted_iota(jnp.int32, counts.shape, 0)
    lane = lax.broadcasted_iota(jnp.int32, counts.shape, 1)
    here = (row == lax.axis_index("head")) & (lane == block_ref[:, : counts.shape[1]])
    live = jnp.sum(jnp.where(here, counts[...].astype(F32), 0.0), axis=1, keepdims=True)
    live = jnp.sum(live, axis=0, keepdims=True).astype(jnp.int32)
    row = lax.broadcasted_iota(jnp.int32, (cap, hd), 0)
    g = jnp.where(row < live, g, 0.0).astype(BF)
    qkv = qkv.astype(BF)[:cap]
    for i in range(NY):
        y_ref[i, :, : 2 * hd] = qkv[:, hd:]
        leave[2 * i + 1].start()
    z_ref[0, :, :hd] = qkv[:, :hd]
    z_ref[0, :, hd:] = g
    for copy in leave:
        copy.wait()


def block_kernel(in_ref, out_ref):
    out_ref[...] = in_ref[...] + (lax.axis_index("z") * NY + lax.axis_index("y"))


def padded(pad_ref, ref, lo, hi):
    n, cap = ref.shape[0], ref.shape[1]
    w = hi - lo
    pad_ref[:, SLOT - 16 :, :] = jnp.zeros((n, 16, w), BF)
    for i in range(n):
        pad_ref[i, :cap, :] = ref[i, :, lo:hi]
    return pad_ref[...].reshape(n * SLOT, w)


def orders(cnt_ref, nz, axis_q):
    z, y, h = (lax.axis_index(a) for a in ("z", "y", "head"))

    def one(n, axis, block_of, dead):
        shape = (n * SLOT, 1) if axis == 0 else (1, n * SLOT)
        at = lax.broadcasted_iota(jnp.int32, shape, axis)
        out = jnp.full(shape, dead, jnp.int32)
        for i in range(n):
            b = block_of(i)
            c = at - i * SLOT
            live = (c >= 0) & (c < cnt_ref[h, b])
            out = jnp.where(live, c + b * SLOT, out)
        return out

    order_q = one(nz, axis_q, lambda i: i * NY + y, -1)
    order_k = one(NY, 1 - axis_q, lambda i: z * NY + i, 1 << 30)
    return order_q, order_k


def split(x):
    hi = x.astype(BF).astype(F32)
    return hi, x - hi


def partial_kernel(scale, cnt_ref, qg_ref, kv_ref, out_ref, qg_pad, kv_pad):
    nz, cap, hd = qg_ref.shape[0], qg_ref.shape[1], qg_ref.shape[2] // 2
    qg = padded(qg_pad, qg_ref, 0, 2 * hd)
    kv = padded(kv_pad, kv_ref, 0, 2 * hd)
    q, g, k, v = qg[:, :hd], qg[:, hd:], kv[:, :hd], kv[:, hd:]
    order_q, order_k = orders(cnt_ref, nz, 0)
    allowed = order_k <= order_q
    s = jnp.where(allowed, mm(q, k, NT) * scale, NEG)
    top = jnp.max(s, axis=1, keepdims=True)
    e = jnp.where(allowed, jnp.exp(s - top), 0.0)
    total = jnp.sum(e, axis=1, keepdims=True)
    total = jnp.where(total > 0.0, total, 1.0)
    p = e * (1.0 / total)
    gp = mm(g, v, NT)
    delta = jnp.sum(p * gp, axis=1, keepdims=True)
    a = mm((p * (gp - delta)).astype(BF), k) * scale
    b = mm(p.astype(BF), k) * scale
    own = jnp.concatenate([a, b], axis=1)
    n = nz * SLOT
    lane = (lax.broadcasted_iota(jnp.int32, (n, 128), 1) - cap) % 4
    stats = jnp.zeros((n, 128), F32)
    for i, col in enumerate(split(top + jnp.log(total)) + split(delta)):
        stats = jnp.where(lane == i, col, stats)
    whole = -(-n // WIDE) * WIDE
    if whole > n:
        stats = jnp.concatenate([stats, jnp.zeros((whole - n, 128), F32)], axis=0)
    stats = stats.T[:SLOT, :]
    row = lax.broadcasted_iota(jnp.int32, (SLOT, WIDE), 0)
    flat = jnp.zeros((SLOT, WIDE), F32)
    for j in range(whole // WIDE):
        flat = jnp.where((row - cap) // 4 == j, stats[:, j * WIDE : (j + 1) * WIDE], flat)
    for i in range(nz):
        out_ref[i] = jnp.where(row < cap, own[i * SLOT : (i + 1) * SLOT, :], flat).astype(BF)


def grads_kernel(
    scale, cnt_ref, qg_ref, kv_ref, st_ref, out_ref, qg_pad, kv_pad, turn
):
    nz, cap, hd = qg_ref.shape[0], qg_ref.shape[1], qg_ref.shape[2] // 2
    n = nz * SLOT
    qg = padded(qg_pad, qg_ref, 0, 2 * hd)
    kv = padded(kv_pad, kv_ref, 0, 2 * hd)
    q, g, k, v = qg[:, :hd], qg[:, hd:], kv[:, :hd], kv[:, hd:]
    chunks = -(-n // WIDE)
    logs, deltas = [], []
    for i in range(nz):
        r = st_ref[i].astype(F32)[cap:]
        line = [jnp.concatenate([r[4 * j + s : 4 * j + s + 1] for j in range(chunks)], axis=1) for s in range(4)]
        logs.append(line[0] + line[1])
        deltas.append(line[2] + line[3])
    top = functools.reduce(jnp.maximum, logs)
    weights = [jnp.exp(x - top) for x in logs]
    total = functools.reduce(jnp.add, weights)
    shares = [w / total for w in weights]
    delta = functools.reduce(jnp.add, [w * d for w, d in zip(shares, deltas)])
    log_total = (top + jnp.log(total))[:, :n]
    width = chunks * WIDE
    lines = shares + [d - delta for d in deltas] + [jnp.zeros((128 - 2 * nz, width), F32)]
    turn[...] = jnp.concatenate(lines, axis=0).T
    delta = delta[:, :n]
    mine = turn[pl.ds(pl.multiple_of(lax.axis_index("z") * SLOT, SLOT), SLOT), :]
    grad_q = jnp.zeros((cap, hd), F32)
    for i in range(nz):
        a = st_ref[i, :cap, :hd].astype(F32)
        b = st_ref[i, :cap, hd:].astype(F32)
        grad_q = grad_q + mine[:cap, i : i + 1] * (a + mine[:cap, nz + i : nz + i + 1] * b)
    order_q, order_k = orders(cnt_ref, nz, 1)
    allowed = order_k <= order_q
    s = mm(k, q, NT) * scale
    p = jnp.where(allowed, jnp.exp(jnp.where(allowed, s - log_total, NEG)), 0.0)
    ds = (p * (mm(v, g, NT) - delta)).astype(BF)
    grad_k = (mm(ds, q) * scale).astype(BF).reshape(NY, SLOT, hd)
    grad_v = mm(p.astype(BF), g).astype(BF).reshape(NY, SLOT, hd)
    grad_q = grad_q.astype(BF)
    for i in range(NY):
        out_ref[i, :, :hd] = grad_k[i, :cap]
        out_ref[i, :, hd : 2 * hd] = grad_v[i, :cap]
        out_ref[i, :, 2 * hd :] = grad_q


def rows_kernel(back_ref, kv_ref, wq_ref, wk_ref, wv_ref, g_ref, t_ref, x_pad, q_pad):
    heads, cap, cols = g_ref.shape
    hd = wq_ref.shape[1]
    kv = jnp.zeros((cap, 2 * hd), F32)
    for i in range(NY):
        kv = kv + back_ref[i, :, : 2 * hd].astype(F32)
    qkv = jnp.concatenate([back_ref[lax.axis_index("y"), :, 2 * hd :], kv.astype(BF)], axis=1)
    x = padded(x_pad, kv_ref, 2 * hd, kv_ref.shape[2])
    grad_q = padded(q_pad, back_ref, 2 * hd, 3 * hd)
    t_ref[...] = mm(x, grad_q, TN).reshape(t_ref.shape).astype(BF)
    for c in range(heads):
        part = pl.ds(c * cols, cols)
        w = jnp.concatenate([wq_ref[part, :], wk_ref[part, :], wv_ref[part, :]], axis=1)
        g_ref[c] = mm(qkv, w, NT).astype(BF)


def finish_kernel(cnt_ref, sel_ref, g_ref, t_ref, h_out, w_out, pad_ref):
    heads, cap, cols = g_ref.shape
    toks = h_out.shape[0]
    block = lax.axis_index("z") * NY + lax.axis_index("y")
    column = sel_ref[...].astype(F32).T
    row = lax.broadcasted_iota(jnp.int32, (SLOT, 1), 0)
    target = []
    for h in range(heads):
        at = column[:SLOT, h : h + 1].astype(jnp.int32)
        target.append(jnp.where(row < cnt_ref[h, block], at, -1))
    target = jnp.concatenate(target, axis=0)
    lane = lax.broadcasted_iota(jnp.int32, (heads * SLOT, toks), 1)
    hit = jnp.where(lane == target, 1.0, 0.0).astype(BF)
    grads = padded(pad_ref, g_ref, 0, cols)
    h_out[...] = mm(hit, grads, TN).astype(BF)
    w_out[...] = jnp.sum(t_ref[...].astype(F32), axis=0)


def body(hidden, upstream, w_query, w_key, w_value, w_output, selected, select_count):
    nz, heads = lax.axis_size("z"), lax.axis_size("head")
    toks, cols = hidden.shape
    hd = w_query.shape[2]
    cap = selected.shape[1] // (nz * NY)
    scale = hd ** (-0.5)
    sds = jax.ShapeDtypeStruct

    def swap(x, axis):
        return lax.all_to_all(x, axis, split_axis=0, concat_axis=0, tiled=True)

    picked, mine = call(
        pick_kernel,
        (sds((heads, 2 * cap, cols), BF), sds((heads, 128), jnp.int32)),
        (selected, hidden, upstream),
        [HBM] * 3,
        [
            pltpu.VMEM((2 * toks, cols), BF),
            pltpu.VMEM((heads, 2 * cap, cols), BF),
            pltpu.VMEM((heads, WIDE), jnp.int32),
            pltpu.SemaphoreType.DMA((7,)),
            pltpu.SemaphoreType.DMA((min(heads, 4),)),
        ],
        limit=54,
        out_specs=(HBM, VMEM),
    )
    picked, block = lax.optimization_barrier((picked, jnp.zeros((heads, 128), jnp.int32)))
    block = pl.pallas_call(
        block_kernel,
        out_shape=sds(block.shape, jnp.int32),
        in_specs=[VMEM],
        out_specs=VMEM,
        compiler_params=pltpu.CompilerParams(vmem_limit_bytes=1 << 20),
        cost_estimate=pl.CostEstimate(flops=10000000000, bytes_accessed=0, transcendentals=0),
    )(block)
    picked, block = lax.optimization_barrier((picked, block))
    rows = swap(picked, "head")
    piece = heads * cols // NY
    to_z, to_y = call(
        functools.partial(project_kernel, nz),
        (sds((1, cap, 2 * hd), BF), sds((NY, cap, 2 * hd + piece), BF)),
        (block, select_count, rows, w_query[0], w_key[0], w_value[0], w_output[0]),
        [VMEM, HBM] + [VMEM] * 5,
        [
            pltpu.VMEM((2 * cap, hd), F32),
            pltpu.VMEM((NY, cap, 2 * hd + piece), BF),
            pltpu.VMEM(select_count.shape, jnp.int32),
            pltpu.SemaphoreType.DMA((2 * NY,)),
            pltpu.SemaphoreType.DMA,
        ],
        limit=16,
        out_specs=(VMEM, HBM),
    )
    count, to_z, to_y = lax.optimization_barrier((select_count, to_z, to_y))
    qg = lax.all_gather(to_z, "z", axis=0, tiled=True)
    kv = swap(to_y, "y")
    pads = [pltpu.VMEM((nz, SLOT, 2 * hd), BF), pltpu.VMEM((NY, SLOT, 2 * hd), BF)]
    part = call(
        functools.partial(partial_kernel, scale),
        sds((nz, SLOT, 2 * hd), BF),
        (count, qg, kv),
        [SMEM] + [VMEM] * 2,
        pads,
    )
    joined = swap(part, "z")
    grads = call(
        functools.partial(grads_kernel, scale),
        sds((NY, cap, 3 * hd), BF),
        (count, qg, kv, joined),
        [SMEM] + [VMEM] * 3,
        pads + [pltpu.VMEM((-(-nz * SLOT // WIDE) * WIDE, 128), F32)],
    )
    back = swap(grads, "y")
    grad_rows, weight_terms = call(
        rows_kernel,
        (sds((heads, cap, cols), BF), sds((nz, piece // nz, hd), BF)),
        (back, kv, w_query[0], w_key[0], w_value[0]),
        [VMEM] * 5,
        [pltpu.VMEM((NY, SLOT, piece), BF), pltpu.VMEM((NY, SLOT, hd), BF)],
    )
    returned, terms = swap(grad_rows, "head"), swap(weight_terms, "z")
    grad_hidden, grad_query = call(
        finish_kernel,
        (sds((toks, cols), BF), sds((piece // nz, hd), F32)),
        (count, mine, returned, terms),
        [SMEM] + [VMEM] * 3,
        [pltpu.VMEM((heads, SLOT, cols), BF)],
    )
    return grad_hidden, grad_query[None]


def solution(mesh):
    seq, heads = mesh.devices.shape
    fine = Mesh(mesh.devices.reshape(seq // NY, NY, heads), ("z", "y", "head"))
    both = ("z", "y")
    weight = P("head", None, None)
    in_specs = (P(both, "head"), P(both, "head"), weight, weight, weight, weight, P(), P())
    out_specs = (P(both, "head"), P("head", both, None))
    return jax.shard_map(body, mesh=fine, in_specs=in_specs, out_specs=out_specs, check_vma=False)
```

```python
import functools

import jax
import jax.numpy as jnp
from jax import lax
from jax.experimental import pallas as pl
from jax.experimental.pallas import tpu as pltpu
from jax.sharding import Mesh, PartitionSpec as P

NY = 8
SLOT = 48
WIDE = 256
NEG = -1e30
BF = jnp.bfloat16
F32 = jnp.float32
VMEM = pl.BlockSpec(memory_space=pltpu.VMEM)
SMEM = pl.BlockSpec(memory_space=pltpu.SMEM)
HBM = pl.BlockSpec(memory_space=pltpu.HBM)
NN = (((1,), (0,)), ((), ()))
NT = (((1,), (1,)), ((), ()))
TN = (((0,), (0,)), ((), ()))


def mm(a, b, dims=NN):
    return lax.dot_general(a, b, dims, preferred_element_type=F32)


def call(kernel, outs, args, specs, scratch=(), limit=16 << 20, out_specs=None, flops=0):
    return pl.pallas_call(
        kernel,
        out_shape=outs,
        in_specs=specs,
        out_specs=out_specs or jax.tree.map(lambda _: VMEM, outs),
        scratch_shapes=list(scratch),
        compiler_params=pltpu.CompilerParams(vmem_limit_bytes=limit),
        cost_estimate=pl.CostEstimate(flops=flops, bytes_accessed=0, transcendentals=0)
        if flops
        else None,
    )(*args)


def pick_kernel(
    sel_ref, hid_ref, up_ref, out_ref, mine_ref, table, ready, view, sems, out_sems
):
    heads, rows, cols = out_ref.shape
    cap, toks = rows // 2, hid_ref.shape[0]
    start = (lax.axis_index("z") * NY + lax.axis_index("y")) * cap
    aligned = jnp.minimum(start // 128 * 128, sel_ref.shape[1] - WIDE)
    window = pltpu.make_async_copy(
        sel_ref.at[:, pl.ds(pl.multiple_of(aligned, 128), WIDE)], view, sems.at[0]
    )
    window.start()
    part = toks // 3
    copies = []
    for i, src in enumerate((hid_ref, up_ref)):
        for j in range(3):
            dst = table.at[pl.ds(i * toks + j * part, part)]
            copies.append(
                pltpu.make_async_copy(src.at[pl.ds(j * part, part)], dst, sems.at[3 * i + j + 1])
            )
    for copy in copies:
        copy.start()
    window.wait()
    shift = lax.rem(WIDE - (start - aligned), WIDE)
    low = pltpu.roll(view[...], shift, 1)[:, :128]
    high = pltpu.roll(low, cap, 1) + toks
    lane = lax.broadcasted_iota(jnp.int32, (heads, 128), 1)
    mine = jnp.where(lane < cap, low, high)
    mine_ref[...] = mine
    sel_t = mine.astype(F32).T
    target = jnp.concatenate([sel_t[:rows, h : h + 1] for h in range(heads)], axis=0)
    target = target.astype(jnp.int32)
    lane = lax.broadcasted_iota(jnp.int32, (heads * rows, 2 * toks), 1)
    onehot = jnp.where(lane == target, 1.0, 0.0).astype(BF)
    for copy in copies:
        copy.wait()
    parts = out_sems.shape[0]
    some = heads // parts
    outs = []
    for i in range(parts):
        got = mm(onehot[i * some * rows : (i + 1) * some * rows], table[...])
        at = pl.ds(i * some, some)
        ready[at] = got.reshape(some, rows, cols).astype(BF)
        outs.append(pltpu.make_async_copy(ready.at[at], out_ref.at[at], out_sems.at[i]))
        outs[i].start()
    for copy in outs:
        copy.wait()


def project_kernel(
    nz, cnt_ref, r_ref, wq_ref, wk_ref, wv_ref, wo_ref, z_ref, y_hbm, acc, y_ref, counts, y_sems, sem
):
    heads, rows, cols = r_ref.shape
    cap, hd = rows // 2, wq_ref.shape[1]
    number = pltpu.make_async_copy(cnt_ref, counts, sem)
    number.start()
    wide = heads * cols // (nz * NY)
    leave = []
    for i in range(NY):
        for at in (pl.ds(2 * hd, nz * wide), pl.ds(0, 2 * hd)):
            sem = y_sems.at[len(leave)]
            leave.append(pltpu.make_async_copy(y_ref.at[i, :, at], y_hbm.at[i, :, at], sem))

    def spread(i):
        chunks = []
        for j in range(nz):
            c, off = divmod((j * NY + i) * wide, cols)
            base = off // 128 * 128
            aligned = r_ref[c, :, base : base + 128]
            chunks.append(aligned[:cap, off - base : off - base + wide])
        y_ref[i, :, 2 * hd :] = jnp.concatenate(chunks, axis=1)
        leave[2 * i].start()

    qkv = jnp.zeros((SLOT, 3 * hd), F32)
    g = jnp.zeros((rows, hd), F32)
    for c in range(heads):
        part = pl.ds(c * cols, cols)
        for i in range(c * NY // heads, (c + 1) * NY // heads):
            spread(i)
        x = r_ref[c]
        w = jnp.concatenate([wq_ref[part, :], wk_ref[part, :], wv_ref[part, :]], axis=1)
        qkv = qkv + mm(x[:SLOT], w)
        g = g + mm(x, wo_ref[:, part], NT)
    acc[...] = g
    g = acc[cap:, :]
    number.wait()
    row = lax.broadcasted_iota(jnp.int32, counts.shape, 0)
    lane = lax.broadcasted_iota(jnp.int32, counts.shape, 1)
    here = (row == lax.axis_index("head")) & (lane == lax.axis_index("z") * NY + lax.axis_index("y"))
    live = jnp.sum(jnp.where(here, counts[...].astype(F32), 0.0), axis=1, keepdims=True)
    live = jnp.sum(live, axis=0, keepdims=True).astype(jnp.int32)
    row = lax.broadcasted_iota(jnp.int32, (cap, hd), 0)
    g = jnp.where(row < live, g, 0.0).astype(BF)
    qkv = qkv.astype(BF)[:cap]
    for i in range(NY):
        y_ref[i, :, : 2 * hd] = qkv[:, hd:]
        leave[2 * i + 1].start()
    z_ref[0, :, :hd] = qkv[:, :hd]
    z_ref[0, :, hd:] = g
    for copy in leave:
        copy.wait()


def padded(pad_ref, ref, lo, hi):
    n, cap = ref.shape[0], ref.shape[1]
    w = hi - lo
    pad_ref[:, SLOT - 16 :, :] = jnp.zeros((n, 16, w), BF)
    for i in range(n):
        pad_ref[i, :cap, :] = ref[i, :, lo:hi]
    return pad_ref[...].reshape(n * SLOT, w)


def orders(cnt_ref, nz, axis_q):
    z, y, h = (lax.axis_index(a) for a in ("z", "y", "head"))

    def one(n, axis, block_of, dead):
        shape = (n * SLOT, 1) if axis == 0 else (1, n * SLOT)
        at = lax.broadcasted_iota(jnp.int32, shape, axis)
        out = jnp.full(shape, dead, jnp.int32)
        for i in range(n):
            b = block_of(i)
            c = at - i * SLOT
            live = (c >= 0) & (c < cnt_ref[h, b])
            out = jnp.where(live, c + b * SLOT, out)
        return out

    order_q = one(nz, axis_q, lambda i: i * NY + y, -1)
    order_k = one(NY, 1 - axis_q, lambda i: z * NY + i, 1 << 30)
    return order_q, order_k


def split(x):
    hi = x.astype(BF).astype(F32)
    return hi, x - hi


def partial_kernel(scale, cnt_ref, qg_ref, kv_ref, out_ref, qg_pad, kv_pad):
    nz, cap, hd = qg_ref.shape[0], qg_ref.shape[1], qg_ref.shape[2] // 2
    qg = padded(qg_pad, qg_ref, 0, 2 * hd)
    kv = padded(kv_pad, kv_ref, 0, 2 * hd)
    q, g, k, v = qg[:, :hd], qg[:, hd:], kv[:, :hd], kv[:, hd:]
    order_q, order_k = orders(cnt_ref, nz, 0)
    allowed = order_k <= order_q
    s = jnp.where(allowed, mm(q, k, NT) * scale, NEG)
    top = jnp.max(s, axis=1, keepdims=True)
    e = jnp.where(allowed, jnp.exp(s - top), 0.0)
    total = jnp.sum(e, axis=1, keepdims=True)
    total = jnp.where(total > 0.0, total, 1.0)
    p = e * (1.0 / total)
    gp = mm(g, v, NT)
    delta = jnp.sum(p * gp, axis=1, keepdims=True)
    a = mm((p * (gp - delta)).astype(BF), k) * scale
    b = mm(p.astype(BF), k) * scale
    own = jnp.concatenate([a, b], axis=1)
    n = nz * SLOT
    lane = (lax.broadcasted_iota(jnp.int32, (n, 128), 1) - cap) % 4
    stats = jnp.zeros((n, 128), F32)
    for i, col in enumerate(split(top + jnp.log(total)) + split(delta)):
        stats = jnp.where(lane == i, col, stats)
    whole = -(-n // WIDE) * WIDE
    if whole > n:
        stats = jnp.concatenate([stats, jnp.zeros((whole - n, 128), F32)], axis=0)
    stats = stats.T[:SLOT, :]
    row = lax.broadcasted_iota(jnp.int32, (SLOT, WIDE), 0)
    flat = jnp.zeros((SLOT, WIDE), F32)
    for j in range(whole // WIDE):
        flat = jnp.where((row - cap) // 4 == j, stats[:, j * WIDE : (j + 1) * WIDE], flat)
    for i in range(nz):
        out_ref[i] = jnp.where(row < cap, own[i * SLOT : (i + 1) * SLOT, :], flat).astype(BF)


def grads_kernel(
    scale, cnt_ref, qg_ref, kv_ref, st_ref, out_ref, qg_pad, kv_pad, turn
):
    nz, cap, hd = qg_ref.shape[0], qg_ref.shape[1], qg_ref.shape[2] // 2
    n = nz * SLOT
    qg = padded(qg_pad, qg_ref, 0, 2 * hd)
    kv = padded(kv_pad, kv_ref, 0, 2 * hd)
    q, g, k, v = qg[:, :hd], qg[:, hd:], kv[:, :hd], kv[:, hd:]
    chunks = -(-n // WIDE)
    logs, deltas = [], []
    for i in range(nz):
        r = st_ref[i].astype(F32)[cap:]
        line = [jnp.concatenate([r[4 * j + s : 4 * j + s + 1] for j in range(chunks)], axis=1) for s in range(4)]
        logs.append(line[0] + line[1])
        deltas.append(line[2] + line[3])
    top = functools.reduce(jnp.maximum, logs)
    weights = [jnp.exp(x - top) for x in logs]
    total = functools.reduce(jnp.add, weights)
    shares = [w / total for w in weights]
    delta = functools.reduce(jnp.add, [w * d for w, d in zip(shares, deltas)])
    log_total = (top + jnp.log(total))[:, :n]
    width = chunks * WIDE
    lines = shares + [d - delta for d in deltas] + [jnp.zeros((128 - 2 * nz, width), F32)]
    turn[...] = jnp.concatenate(lines, axis=0).T
    delta = delta[:, :n]
    mine = turn[pl.ds(pl.multiple_of(lax.axis_index("z") * SLOT, SLOT), SLOT), :]
    grad_q = jnp.zeros((cap, hd), F32)
    for i in range(nz):
        a = st_ref[i, :cap, :hd].astype(F32)
        b = st_ref[i, :cap, hd:].astype(F32)
        grad_q = grad_q + mine[:cap, i : i + 1] * (a + mine[:cap, nz + i : nz + i + 1] * b)
    order_q, order_k = orders(cnt_ref, nz, 1)
    allowed = order_k <= order_q
    s = mm(k, q, NT) * scale
    p = jnp.where(allowed, jnp.exp(jnp.where(allowed, s - log_total, NEG)), 0.0)
    ds = (p * (mm(v, g, NT) - delta)).astype(BF)
    grad_k = (mm(ds, q) * scale).astype(BF).reshape(NY, SLOT, hd)
    grad_v = mm(p.astype(BF), g).astype(BF).reshape(NY, SLOT, hd)
    grad_q = grad_q.astype(BF)
    for i in range(NY):
        out_ref[i, :, :hd] = grad_k[i, :cap]
        out_ref[i, :, hd : 2 * hd] = grad_v[i, :cap]
        out_ref[i, :, 2 * hd :] = grad_q


def rows_kernel(back_ref, kv_ref, wq_ref, wk_ref, wv_ref, g_ref, t_ref, x_pad, q_pad):
    heads, cap, cols = g_ref.shape
    hd = wq_ref.shape[1]
    kv = jnp.zeros((cap, 2 * hd), F32)
    for i in range(NY):
        kv = kv + back_ref[i, :, : 2 * hd].astype(F32)
    qkv = jnp.concatenate([back_ref[lax.axis_index("y"), :, 2 * hd :], kv.astype(BF)], axis=1)
    x = padded(x_pad, kv_ref, 2 * hd, kv_ref.shape[2])
    grad_q = padded(q_pad, back_ref, 2 * hd, 3 * hd)
    t_ref[...] = mm(x, grad_q, TN).reshape(t_ref.shape).astype(BF)
    for c in range(heads):
        part = pl.ds(c * cols, cols)
        w = jnp.concatenate([wq_ref[part, :], wk_ref[part, :], wv_ref[part, :]], axis=1)
        g_ref[c] = mm(qkv, w, NT).astype(BF)


def finish_kernel(cnt_ref, sel_ref, g_ref, t_ref, h_out, w_out, pad_ref):
    heads, cap, cols = g_ref.shape
    toks = h_out.shape[0]
    block = lax.axis_index("z") * NY + lax.axis_index("y")
    column = sel_ref[...].astype(F32).T
    row = lax.broadcasted_iota(jnp.int32, (SLOT, 1), 0)
    target = []
    for h in range(heads):
        at = column[:SLOT, h : h + 1].astype(jnp.int32)
        target.append(jnp.where(row < cnt_ref[h, block], at, -1))
    target = jnp.concatenate(target, axis=0)
    lane = lax.broadcasted_iota(jnp.int32, (heads * SLOT, toks), 1)
    hit = jnp.where(lane == target, 1.0, 0.0).astype(BF)
    grads = padded(pad_ref, g_ref, 0, cols)
    h_out[...] = mm(hit, grads, TN).astype(BF)
    w_out[...] = jnp.sum(t_ref[...].astype(F32), axis=0)


def body(hidden, upstream, w_query, w_key, w_value, w_output, selected, select_count):
    nz, heads = lax.axis_size("z"), lax.axis_size("head")
    toks, cols = hidden.shape
    hd = w_query.shape[2]
    cap = selected.shape[1] // (nz * NY)
    scale = hd ** (-0.5)
    sds = jax.ShapeDtypeStruct

    def swap(x, axis):
        return lax.all_to_all(x, axis, split_axis=0, concat_axis=0, tiled=True)

    picked, mine = call(
        pick_kernel,
        (sds((heads, 2 * cap, cols), BF), sds((heads, 128), jnp.int32)),
        (selected, hidden, upstream),
        [HBM] * 3,
        [
            pltpu.VMEM((2 * toks, cols), BF),
            pltpu.VMEM((heads, 2 * cap, cols), BF),
            pltpu.VMEM((heads, WIDE), jnp.int32),
            pltpu.SemaphoreType.DMA((7,)),
            pltpu.SemaphoreType.DMA((min(heads, 4),)),
        ],
        limit=54 << 20,
        flops=20000000000,
        out_specs=(HBM, VMEM),
    )
    rows = swap(picked, "head")
    piece = heads * cols // NY
    to_z, to_y = call(
        functools.partial(project_kernel, nz),
        (sds((1, cap, 2 * hd), BF), sds((NY, cap, 2 * hd + piece), BF)),
        (select_count, rows, w_query[0], w_key[0], w_value[0], w_output[0]),
        [HBM] + [VMEM] * 5,
        [
            pltpu.VMEM((2 * cap, hd), F32),
            pltpu.VMEM((NY, cap, 2 * hd + piece), BF),
            pltpu.VMEM(select_count.shape, jnp.int32),
            pltpu.SemaphoreType.DMA((2 * NY,)),
            pltpu.SemaphoreType.DMA,
        ],
        out_specs=(VMEM, HBM),
    )
    count, to_z, to_y = lax.optimization_barrier((select_count, to_z, to_y))
    qg = lax.all_gather(to_z, "z", axis=0, tiled=True)
    kv = swap(to_y, "y")
    pads = [pltpu.VMEM((nz, SLOT, 2 * hd), BF), pltpu.VMEM((NY, SLOT, 2 * hd), BF)]
    part = call(
        functools.partial(partial_kernel, scale),
        sds((nz, SLOT, 2 * hd), BF),
        (count, qg, kv),
        [SMEM] + [VMEM] * 2,
        pads,
    )
    joined = swap(part, "z")
    grads = call(
        functools.partial(grads_kernel, scale),
        sds((NY, cap, 3 * hd), BF),
        (count, qg, kv, joined),
        [SMEM] + [VMEM] * 3,
        pads + [pltpu.VMEM((-(-nz * SLOT // WIDE) * WIDE, 128), F32)],
    )
    back = swap(grads, "y")
    grad_rows, weight_terms = call(
        rows_kernel,
        (sds((heads, cap, cols), BF), sds((nz, piece // nz, hd), BF)),
        (back, kv, w_query[0], w_key[0], w_value[0]),
        [VMEM] * 5,
        [pltpu.VMEM((NY, SLOT, piece), BF), pltpu.VMEM((NY, SLOT, hd), BF)],
    )
    returned, terms = swap(grad_rows, "head"), swap(weight_terms, "z")
    grad_hidden, grad_query = call(
        finish_kernel,
        (sds((toks, cols), BF), sds((piece // nz, hd), F32)),
        (count, mine, returned, terms),
        [SMEM] + [VMEM] * 3,
        [pltpu.VMEM((heads, SLOT, cols), BF)],
    )
    return grad_hidden, grad_query[None]


def solution(mesh):
    seq, heads = mesh.devices.shape
    fine = Mesh(mesh.devices.reshape(seq // NY, NY, heads), ("z", "y", "head"))
    both = ("z", "y")
    weight = P("head", None, None)
    in_specs = (P(both, "head"), P(both, "head"), weight, weight, weight, weight, P(), P())
    out_specs = (P(both, "head"), P("head", both, None))
    return jax.shard_map(body, mesh=fine, in_specs=in_specs, out_specs=out_specs, check_vma=False)
```

```python
import functools

import jax
import jax.numpy as jnp
from jax import lax
from jax.experimental import pallas as pl
from jax.experimental.pallas import tpu as pltpu
from jax.sharding import Mesh, PartitionSpec as P

NY = 8
SLOT = 48
WIDE = 256
NEG = -1e30
BF = jnp.bfloat16
F32 = jnp.float32
VMEM = pl.BlockSpec(memory_space=pltpu.VMEM)
SMEM = pl.BlockSpec(memory_space=pltpu.SMEM)
HBM = pl.BlockSpec(memory_space=pltpu.HBM)
NN = (((1,), (0,)), ((), ()))
NT = (((1,), (1,)), ((), ()))
TN = (((0,), (0,)), ((), ()))


def mm(a, b, dims=NN):
    return lax.dot_general(a, b, dims, preferred_element_type=F32)


def call(kernel, outs, args, specs, scratch=(), limit=16 << 20, out_specs=None, flops=0):
    return pl.pallas_call(
        kernel,
        out_shape=outs,
        in_specs=specs,
        out_specs=out_specs or jax.tree.map(lambda _: VMEM, outs),
        scratch_shapes=list(scratch),
        compiler_params=pltpu.CompilerParams(vmem_limit_bytes=limit),
        cost_estimate=pl.CostEstimate(flops=flops, bytes_accessed=0, transcendentals=0)
        if flops
        else None,
    )(*args)


def pick_kernel(
    sel_ref, hid_ref, up_ref, out_ref, mine_ref, table, ready, view, sems, out_sems
):
    heads, rows, cols = out_ref.shape
    cap, toks = rows // 2, hid_ref.shape[0]
    start = (lax.axis_index("z") * NY + lax.axis_index("y")) * cap
    aligned = jnp.minimum(start // 128 * 128, sel_ref.shape[1] - WIDE)
    window = pltpu.make_async_copy(
        sel_ref.at[:, pl.ds(pl.multiple_of(aligned, 128), WIDE)], view, sems.at[0]
    )
    window.start()
    part = toks // 3
    copies = []
    for i, src in enumerate((hid_ref, up_ref)):
        for j in range(3):
            dst = table.at[pl.ds(i * toks + j * part, part)]
            copies.append(
                pltpu.make_async_copy(src.at[pl.ds(j * part, part)], dst, sems.at[3 * i + j + 1])
            )
    for copy in copies:
        copy.start()
    window.wait()
    shift = lax.rem(WIDE - (start - aligned), WIDE)
    low = pltpu.roll(view[...], shift, 1)[:, :128]
    high = pltpu.roll(low, cap, 1) + toks
    lane = lax.broadcasted_iota(jnp.int32, (heads, 128), 1)
    mine = jnp.where(lane < cap, low, high)
    mine_ref[...] = mine
    sel_t = mine.astype(F32).T
    target = jnp.concatenate([sel_t[:rows, h : h + 1] for h in range(heads)], axis=0)
    target = target.astype(jnp.int32)
    lane = lax.broadcasted_iota(jnp.int32, (heads * rows, 2 * toks), 1)
    onehot = jnp.where(lane == target, 1.0, 0.0).astype(BF)
    for copy in copies:
        copy.wait()
    parts = out_sems.shape[0]
    some = heads // parts
    outs = []
    for i in range(parts):
        got = mm(onehot[i * some * rows : (i + 1) * some * rows], table[...])
        at = pl.ds(i * some, some)
        ready[at] = got.reshape(some, rows, cols).astype(BF)
        outs.append(pltpu.make_async_copy(ready.at[at], out_ref.at[at], out_sems.at[i]))
        outs[i].start()
    for copy in outs:
        copy.wait()


def project_kernel(
    nz, cnt_ref, r_ref, wq_ref, wk_ref, wv_ref, wo_ref, z_ref, y_hbm, acc, y_ref, counts, y_sems, sem
):
    heads, rows, cols = r_ref.shape
    cap, hd = rows // 2, wq_ref.shape[1]
    number = pltpu.make_async_copy(cnt_ref, counts, sem)
    number.start()
    wide = heads * cols // (nz * NY)
    leave = []
    for i in range(NY):
        for at in (pl.ds(2 * hd, nz * wide), pl.ds(0, 2 * hd)):
            sem = y_sems.at[len(leave)]
            leave.append(pltpu.make_async_copy(y_ref.at[i, :, at], y_hbm.at[i, :, at], sem))

    def spread(i):
        chunks = []
        for j in range(nz):
            c, off = divmod((j * NY + i) * wide, cols)
            base = off // 128 * 128
            aligned = r_ref[c, :, base : base + 128]
            chunks.append(aligned[:cap, off - base : off - base + wide])
        y_ref[i, :, 2 * hd :] = jnp.concatenate(chunks, axis=1)
        leave[2 * i].start()

    qkv = jnp.zeros((SLOT, 3 * hd), F32)
    g = jnp.zeros((rows, hd), F32)
    for c in range(heads):
        part = pl.ds(c * cols, cols)
        for i in range(c * NY // heads, (c + 1) * NY // heads):
            spread(i)
        x = r_ref[c]
        w = jnp.concatenate([wq_ref[part, :], wk_ref[part, :], wv_ref[part, :]], axis=1)
        qkv = qkv + mm(x[:SLOT], w)
        g = g + mm(x, wo_ref[:, part], NT)
    acc[...] = g
    g = acc[cap:, :]
    number.wait()
    row = lax.broadcasted_iota(jnp.int32, counts.shape, 0)
    lane = lax.broadcasted_iota(jnp.int32, counts.shape, 1)
    here = (row == lax.axis_index("head")) & (lane == lax.axis_index("z") * NY + lax.axis_index("y"))
    live = jnp.sum(jnp.where(here, counts[...].astype(F32), 0.0), axis=1, keepdims=True)
    live = jnp.sum(live, axis=0, keepdims=True).astype(jnp.int32)
    row = lax.broadcasted_iota(jnp.int32, (cap, hd), 0)
    g = jnp.where(row < live, g, 0.0).astype(BF)
    qkv = qkv.astype(BF)[:cap]
    for i in range(NY):
        y_ref[i, :, : 2 * hd] = qkv[:, hd:]
        leave[2 * i + 1].start()
    z_ref[0, :, :hd] = qkv[:, :hd]
    z_ref[0, :, hd:] = g
    for copy in leave:
        copy.wait()


def padded(pad_ref, ref, lo, hi):
    n, cap = ref.shape[0], ref.shape[1]
    w = hi - lo
    pad_ref[:, SLOT - 16 :, :] = jnp.zeros((n, 16, w), BF)
    for i in range(n):
        pad_ref[i, :cap, :] = ref[i, :, lo:hi]
    return pad_ref[...].reshape(n * SLOT, w)


def orders(cnt_ref, nz, axis_q):
    z, y, h = (lax.axis_index(a) for a in ("z", "y", "head"))

    def one(n, axis, block_of, dead):
        shape = (n * SLOT, 1) if axis == 0 else (1, n * SLOT)
        at = lax.broadcasted_iota(jnp.int32, shape, axis)
        out = jnp.full(shape, dead, jnp.int32)
        for i in range(n):
            b = block_of(i)
            c = at - i * SLOT
            live = (c >= 0) & (c < cnt_ref[h, b])
            out = jnp.where(live, c + b * SLOT, out)
        return out

    order_q = one(nz, axis_q, lambda i: i * NY + y, -1)
    order_k = one(NY, 1 - axis_q, lambda i: z * NY + i, 1 << 30)
    return order_q, order_k


def split(x):
    hi = x.astype(BF).astype(F32)
    return hi, x - hi


def partial_kernel(scale, cnt_ref, qg_ref, kv_ref, out_ref, qg_pad, kv_pad):
    nz, cap, hd = qg_ref.shape[0], qg_ref.shape[1], qg_ref.shape[2] // 2
    qg = padded(qg_pad, qg_ref, 0, 2 * hd)
    kv = padded(kv_pad, kv_ref, 0, 2 * hd)
    q, g, k, v = qg[:, :hd], qg[:, hd:], kv[:, :hd], kv[:, hd:]
    order_q, order_k = orders(cnt_ref, nz, 0)
    allowed = order_k <= order_q
    s = jnp.where(allowed, mm(q, k, NT) * scale, NEG)
    top = jnp.max(s, axis=1, keepdims=True)
    e = jnp.where(allowed, jnp.exp(s - top), 0.0)
    total = jnp.sum(e, axis=1, keepdims=True)
    total = jnp.where(total > 0.0, total, 1.0)
    p = e * (1.0 / total)
    gp = mm(g, v, NT)
    delta = jnp.sum(p * gp, axis=1, keepdims=True)
    a = mm((p * (gp - delta)).astype(BF), k) * scale
    b = mm(p.astype(BF), k) * scale
    own = jnp.concatenate([a, b], axis=1)
    n = nz * SLOT
    lane = (lax.broadcasted_iota(jnp.int32, (n, 128), 1) - cap) % 4
    stats = jnp.zeros((n, 128), F32)
    for i, col in enumerate(split(top + jnp.log(total)) + split(delta)):
        stats = jnp.where(lane == i, col, stats)
    whole = -(-n // WIDE) * WIDE
    if whole > n:
        stats = jnp.concatenate([stats, jnp.zeros((whole - n, 128), F32)], axis=0)
    stats = stats.T[:SLOT, :]
    row = lax.broadcasted_iota(jnp.int32, (SLOT, WIDE), 0)
    flat = jnp.zeros((SLOT, WIDE), F32)
    for j in range(whole // WIDE):
        flat = jnp.where((row - cap) // 4 == j, stats[:, j * WIDE : (j + 1) * WIDE], flat)
    for i in range(nz):
        out_ref[i] = jnp.where(row < cap, own[i * SLOT : (i + 1) * SLOT, :], flat).astype(BF)


def grads_kernel(
    scale, cnt_ref, qg_ref, kv_ref, st_ref, out_ref, qg_pad, kv_pad, turn
):
    nz, cap, hd = qg_ref.shape[0], qg_ref.shape[1], qg_ref.shape[2] // 2
    n = nz * SLOT
    qg = padded(qg_pad, qg_ref, 0, 2 * hd)
    kv = padded(kv_pad, kv_ref, 0, 2 * hd)
    q, g, k, v = qg[:, :hd], qg[:, hd:], kv[:, :hd], kv[:, hd:]
    chunks = -(-n // WIDE)
    logs, deltas = [], []
    for i in range(nz):
        r = st_ref[i].astype(F32)[cap:]
        line = [jnp.concatenate([r[4 * j + s : 4 * j + s + 1] for j in range(chunks)], axis=1) for s in range(4)]
        logs.append(line[0] + line[1])
        deltas.append(line[2] + line[3])
    top = functools.reduce(jnp.maximum, logs)
    weights = [jnp.exp(x - top) for x in logs]
    total = functools.reduce(jnp.add, weights)
    shares = [w / total for w in weights]
    delta = functools.reduce(jnp.add, [w * d for w, d in zip(shares, deltas)])
    log_total = (top + jnp.log(total))[:, :n]
    width = chunks * WIDE
    lines = shares + [d - delta for d in deltas] + [jnp.zeros((128 - 2 * nz, width), F32)]
    turn[...] = jnp.concatenate(lines, axis=0).T
    delta = delta[:, :n]
    mine = turn[pl.ds(pl.multiple_of(lax.axis_index("z") * SLOT, SLOT), SLOT), :]
    grad_q = jnp.zeros((cap, hd), F32)
    for i in range(nz):
        a = st_ref[i, :cap, :hd].astype(F32)
        b = st_ref[i, :cap, hd:].astype(F32)
        grad_q = grad_q + mine[:cap, i : i + 1] * (a + mine[:cap, nz + i : nz + i + 1] * b)
    order_q, order_k = orders(cnt_ref, nz, 1)
    allowed = order_k <= order_q
    s = mm(k, q, NT) * scale
    p = jnp.where(allowed, jnp.exp(jnp.where(allowed, s - log_total, NEG)), 0.0)
    ds = (p * (mm(v, g, NT) - delta)).astype(BF)
    grad_k = (mm(ds, q) * scale).astype(BF).reshape(NY, SLOT, hd)
    grad_v = mm(p.astype(BF), g).astype(BF).reshape(NY, SLOT, hd)
    grad_q = grad_q.astype(BF)
    for i in range(NY):
        out_ref[i, :, :hd] = grad_k[i, :cap]
        out_ref[i, :, hd : 2 * hd] = grad_v[i, :cap]
        out_ref[i, :, 2 * hd :] = grad_q


def rows_kernel(back_ref, kv_ref, wq_ref, wk_ref, wv_ref, g_ref, t_ref, x_pad, q_pad):
    heads, cap, cols = g_ref.shape
    hd = wq_ref.shape[1]
    kv = jnp.zeros((cap, 2 * hd), F32)
    for i in range(NY):
        kv = kv + back_ref[i, :, : 2 * hd].astype(F32)
    qkv = jnp.concatenate([back_ref[lax.axis_index("y"), :, 2 * hd :], kv.astype(BF)], axis=1)
    x = padded(x_pad, kv_ref, 2 * hd, kv_ref.shape[2])
    grad_q = padded(q_pad, back_ref, 2 * hd, 3 * hd)
    t_ref[...] = mm(x, grad_q, TN).reshape(t_ref.shape).astype(BF)
    for c in range(heads):
        part = pl.ds(c * cols, cols)
        w = jnp.concatenate([wq_ref[part, :], wk_ref[part, :], wv_ref[part, :]], axis=1)
        g_ref[c] = mm(qkv, w, NT).astype(BF)


def finish_kernel(cnt_ref, sel_ref, g_ref, t_ref, h_out, w_out, pad_ref):
    heads, cap, cols = g_ref.shape
    toks = h_out.shape[0]
    block = lax.axis_index("z") * NY + lax.axis_index("y")
    column = sel_ref[...].astype(F32).T
    row = lax.broadcasted_iota(jnp.int32, (SLOT, 1), 0)
    target = []
    for h in range(heads):
        at = column[:SLOT, h : h + 1].astype(jnp.int32)
        target.append(jnp.where(row < cnt_ref[h, block], at, -1))
    target = jnp.concatenate(target, axis=0)
    lane = lax.broadcasted_iota(jnp.int32, (heads * SLOT, toks), 1)
    hit = jnp.where(lane == target, 1.0, 0.0).astype(BF)
    grads = padded(pad_ref, g_ref, 0, cols)
    h_out[...] = mm(hit, grads, TN).astype(BF)
    w_out[...] = jnp.sum(t_ref[...].astype(F32), axis=0)


def body(hidden, upstream, w_query, w_key, w_value, w_output, selected, select_count):
    nz, heads = lax.axis_size("z"), lax.axis_size("head")
    toks, cols = hidden.shape
    hd = w_query.shape[2]
    cap = selected.shape[1] // (nz * NY)
    scale = hd ** (-0.5)
    sds = jax.ShapeDtypeStruct

    def swap(x, axis):
        return lax.all_to_all(x, axis, split_axis=0, concat_axis=0, tiled=True)

    picked, mine = call(
        pick_kernel,
        (sds((heads, 2 * cap, cols), BF), sds((heads, 128), jnp.int32)),
        (selected, hidden, upstream),
        [HBM] * 3,
        [
            pltpu.VMEM((2 * toks, cols), BF),
            pltpu.VMEM((heads, 2 * cap, cols), BF),
            pltpu.VMEM((heads, WIDE), jnp.int32),
            pltpu.SemaphoreType.DMA((7,)),
            pltpu.SemaphoreType.DMA((min(heads, 4),)),
        ],
        limit=54 << 20,
        flops=20000000000,
        out_specs=(HBM, VMEM),
    )
    rows = swap(picked, "head")
    piece = heads * cols // NY
    to_z, to_y = call(
        functools.partial(project_kernel, nz),
        (sds((1, cap, 2 * hd), BF), sds((NY, cap, 2 * hd + piece), BF)),
        (select_count, rows, w_query[0], w_key[0], w_value[0], w_output[0]),
        [HBM] + [VMEM] * 5,
        [
            pltpu.VMEM((2 * cap, hd), F32),
            pltpu.VMEM((NY, cap, 2 * hd + piece), BF),
            pltpu.VMEM(select_count.shape, jnp.int32),
            pltpu.SemaphoreType.DMA((2 * NY,)),
            pltpu.SemaphoreType.DMA,
        ],
        out_specs=(VMEM, HBM),
    )
    count, to_z, to_y = lax.optimization_barrier((select_count, to_z, to_y))
    qg = lax.all_gather(to_z, "z", axis=0, tiled=True)
    kv = swap(to_y, "y")
    pads = [pltpu.VMEM((nz, SLOT, 2 * hd), BF), pltpu.VMEM((NY, SLOT, 2 * hd), BF)]
    part = call(
        functools.partial(partial_kernel, scale),
        sds((nz, SLOT, 2 * hd), BF),
        (count, qg, kv),
        [SMEM] + [VMEM] * 2,
        pads,
    )
    joined = swap(part, "z")
    grads = call(
        functools.partial(grads_kernel, scale),
        sds((NY, cap, 3 * hd), BF),
        (count, qg, kv, joined),
        [SMEM] + [VMEM] * 3,
        pads + [pltpu.VMEM((-(-nz * SLOT // WIDE) * WIDE, 128), F32)],
    )
    back = swap(grads, "y")
    grad_rows, weight_terms = call(
        rows_kernel,
        (sds((heads, cap, cols), BF), sds((nz, piece // nz, hd), BF)),
        (back, kv, w_query[0], w_key[0], w_value[0]),
        [VMEM] * 5,
        [pltpu.VMEM((NY, SLOT, piece), BF), pltpu.VMEM((NY, SLOT, hd), BF)],
    )
    terms = swap(weight_terms, "z")
    grad_rows, terms = lax.optimization_barrier((grad_rows, terms))
    returned = swap(grad_rows, "head")
    grad_hidden, grad_query = call(
        finish_kernel,
        (sds((toks, cols), BF), sds((piece // nz, hd), F32)),
        (count, mine, returned, terms),
        [SMEM] + [VMEM] * 3,
        [pltpu.VMEM((heads, SLOT, cols), BF)],
    )
    return grad_hidden, grad_query[None]


def solution(mesh):
    seq, heads = mesh.devices.shape
    fine = Mesh(mesh.devices.reshape(seq // NY, NY, heads), ("z", "y", "head"))
    both = ("z", "y")
    weight = P("head", None, None)
    in_specs = (P(both, "head"), P(both, "head"), weight, weight, weight, weight, P(), P())
    out_specs = (P(both, "head"), P("head", both, None))
    return jax.shard_map(body, mesh=fine, in_specs=in_specs, out_specs=out_specs, check_vma=False)
```

```python
import functools

import jax
import jax.numpy as jnp
from jax import lax
from jax.experimental import pallas as pl
from jax.experimental.pallas import tpu as pltpu
from jax.sharding import Mesh, PartitionSpec as P

NY = 8
SLOT = 48
WIDE = 256
NEG = -1e30
BF = jnp.bfloat16
F32 = jnp.float32
VMEM = pl.BlockSpec(memory_space=pltpu.VMEM)
SMEM = pl.BlockSpec(memory_space=pltpu.SMEM)
HBM = pl.BlockSpec(memory_space=pltpu.HBM)
NN = (((1,), (0,)), ((), ()))
NT = (((1,), (1,)), ((), ()))
TN = (((0,), (0,)), ((), ()))


def mm(a, b, dims=NN):
    return lax.dot_general(a, b, dims, preferred_element_type=F32)


def call(kernel, outs, args, specs, scratch=(), limit=16 << 20, out_specs=None, flops=0):
    return pl.pallas_call(
        kernel,
        out_shape=outs,
        in_specs=specs,
        out_specs=out_specs or jax.tree.map(lambda _: VMEM, outs),
        scratch_shapes=list(scratch),
        compiler_params=pltpu.CompilerParams(vmem_limit_bytes=limit),
        cost_estimate=pl.CostEstimate(flops=flops, bytes_accessed=0, transcendentals=0)
        if flops
        else None,
    )(*args)


def pick_kernel(
    sel_ref, hid_ref, up_ref, out_ref, mine_ref, table, ready, view, sems, out_sems
):
    heads, rows, cols = out_ref.shape
    cap, toks = rows // 2, hid_ref.shape[0]
    start = (lax.axis_index("z") * NY + lax.axis_index("y")) * cap
    aligned = jnp.minimum(start // 128 * 128, sel_ref.shape[1] - WIDE)
    window = pltpu.make_async_copy(
        sel_ref.at[:, pl.ds(pl.multiple_of(aligned, 128), WIDE)], view, sems.at[0]
    )
    window.start()
    part = toks // 3
    copies = []
    for i, src in enumerate((hid_ref, up_ref)):
        for j in range(3):
            dst = table.at[pl.ds(i * toks + j * part, part)]
            copies.append(
                pltpu.make_async_copy(src.at[pl.ds(j * part, part)], dst, sems.at[3 * i + j + 1])
            )
    for copy in copies:
        copy.start()
    window.wait()
    shift = lax.rem(WIDE - (start - aligned), WIDE)
    low = pltpu.roll(view[...], shift, 1)[:, :128]
    high = pltpu.roll(low, cap, 1) + toks
    lane = lax.broadcasted_iota(jnp.int32, (heads, 128), 1)
    mine = jnp.where(lane < cap, low, high)
    mine_ref[...] = mine
    sel_t = mine.astype(F32).T
    target = jnp.concatenate([sel_t[:rows, h : h + 1] for h in range(heads)], axis=0)
    target = target.astype(jnp.int32)
    lane = lax.broadcasted_iota(jnp.int32, (heads * rows, 2 * toks), 1)
    onehot = jnp.where(lane == target, 1.0, 0.0).astype(BF)
    for copy in copies:
        copy.wait()
    parts = out_sems.shape[0]
    some = heads // parts
    outs = []
    for i in range(parts):
        got = mm(onehot[i * some * rows : (i + 1) * some * rows], table[...])
        at = pl.ds(i * some, some)
        ready[at] = got.reshape(some, rows, cols).astype(BF)
        outs.append(pltpu.make_async_copy(ready.at[at], out_ref.at[at], out_sems.at[i]))
        outs[i].start()
    for copy in outs:
        copy.wait()


def project_kernel(
    nz, cnt_ref, r_ref, wq_ref, wk_ref, wv_ref, wo_ref, z_ref, y_hbm, acc, y_ref, counts, y_sems, sem
):
    heads, rows, cols = r_ref.shape
    cap, hd = rows // 2, wq_ref.shape[1]
    number = pltpu.make_async_copy(cnt_ref, counts, sem)
    number.start()
    wide = heads * cols // (nz * NY)
    leave = []
    for i in range(NY):
        for at in (pl.ds(2 * hd, nz * wide), pl.ds(0, 2 * hd)):
            sem = y_sems.at[len(leave)]
            leave.append(pltpu.make_async_copy(y_ref.at[i, :, at], y_hbm.at[i, :, at], sem))

    def spread(i):
        chunks = []
        for j in range(nz):
            c, off = divmod((j * NY + i) * wide, cols)
            base = off // 128 * 128
            aligned = r_ref[c, :, base : base + 128]
            chunks.append(aligned[:cap, off - base : off - base + wide])
        y_ref[i, :, 2 * hd :] = jnp.concatenate(chunks, axis=1)
        leave[2 * i].start()

    qkv = jnp.zeros((SLOT, 3 * hd), F32)
    g = jnp.zeros((rows, hd), F32)
    for c in range(heads):
        part = pl.ds(c * cols, cols)
        for i in range(c * NY // heads, (c + 1) * NY // heads):
            spread(i)
        x = r_ref[c]
        w = jnp.concatenate([wq_ref[part, :], wk_ref[part, :], wv_ref[part, :]], axis=1)
        qkv = qkv + mm(x[:SLOT], w)
        g = g + mm(x, wo_ref[:, part], NT)
    acc[...] = g
    g = acc[cap:, :]
    number.wait()
    row = lax.broadcasted_iota(jnp.int32, counts.shape, 0)
    lane = lax.broadcasted_iota(jnp.int32, counts.shape, 1)
    here = (row == lax.axis_index("head")) & (lane == lax.axis_index("z") * NY + lax.axis_index("y"))
    live = jnp.sum(jnp.where(here, counts[...].astype(F32), 0.0), axis=1, keepdims=True)
    live = jnp.sum(live, axis=0, keepdims=True).astype(jnp.int32)
    row = lax.broadcasted_iota(jnp.int32, (cap, hd), 0)
    g = jnp.where(row < live, g, 0.0).astype(BF)
    qkv = qkv.astype(BF)[:cap]
    for i in range(NY):
        y_ref[i, :, : 2 * hd] = qkv[:, hd:]
        leave[2 * i + 1].start()
    z_ref[0, :, :hd] = qkv[:, :hd]
    z_ref[0, :, hd:] = g
    for copy in leave:
        copy.wait()


def padded(pad_ref, ref, lo, hi):
    n, cap = ref.shape[0], ref.shape[1]
    w = hi - lo
    pad_ref[:, SLOT - 16 :, :] = jnp.zeros((n, 16, w), BF)
    for i in range(n):
        pad_ref[i, :cap, :] = ref[i, :, lo:hi]
    return pad_ref[...].reshape(n * SLOT, w)


def orders(cnt_ref, nz, axis_q):
    z, y, h = (lax.axis_index(a) for a in ("z", "y", "head"))

    def one(n, axis, block_of, dead):
        shape = (n * SLOT, 1) if axis == 0 else (1, n * SLOT)
        at = lax.broadcasted_iota(jnp.int32, shape, axis)
        out = jnp.full(shape, dead, jnp.int32)
        for i in range(n):
            b = block_of(i)
            c = at - i * SLOT
            live = (c >= 0) & (c < cnt_ref[h, b])
            out = jnp.where(live, c + b * SLOT, out)
        return out

    order_q = one(nz, axis_q, lambda i: i * NY + y, -1)
    order_k = one(NY, 1 - axis_q, lambda i: z * NY + i, 1 << 30)
    return order_q, order_k


def split(x):
    hi = x.astype(BF).astype(F32)
    return hi, x - hi


def partial_kernel(scale, cnt_ref, qg_ref, kv_ref, out_ref, qg_pad, kv_pad):
    nz, cap, hd = qg_ref.shape[0], qg_ref.shape[1], qg_ref.shape[2] // 2
    qg = padded(qg_pad, qg_ref, 0, 2 * hd)
    kv = padded(kv_pad, kv_ref, 0, 2 * hd)
    q, g, k, v = qg[:, :hd], qg[:, hd:], kv[:, :hd], kv[:, hd:]
    order_q, order_k = orders(cnt_ref, nz, 0)
    allowed = order_k <= order_q
    s = jnp.where(allowed, mm(q, k, NT) * scale, NEG)
    top = jnp.max(s, axis=1, keepdims=True)
    e = jnp.where(allowed, jnp.exp(s - top), 0.0)
    total = jnp.sum(e, axis=1, keepdims=True)
    total = jnp.where(total > 0.0, total, 1.0)
    p = e * (1.0 / total)
    gp = mm(g, v, NT)
    delta = jnp.sum(p * gp, axis=1, keepdims=True)
    a = mm((p * (gp - delta)).astype(BF), k) * scale
    b = mm(p.astype(BF), k) * scale
    own = jnp.concatenate([a, b], axis=1)
    n = nz * SLOT
    lane = (lax.broadcasted_iota(jnp.int32, (n, 128), 1) - cap) % 4
    stats = jnp.zeros((n, 128), F32)
    for i, col in enumerate(split(top + jnp.log(total)) + split(delta)):
        stats = jnp.where(lane == i, col, stats)
    whole = -(-n // WIDE) * WIDE
    if whole > n:
        stats = jnp.concatenate([stats, jnp.zeros((whole - n, 128), F32)], axis=0)
    stats = stats.T[:SLOT, :]
    row = lax.broadcasted_iota(jnp.int32, (SLOT, WIDE), 0)
    flat = jnp.zeros((SLOT, WIDE), F32)
    for j in range(whole // WIDE):
        flat = jnp.where((row - cap) // 4 == j, stats[:, j * WIDE : (j + 1) * WIDE], flat)
    for i in range(nz):
        out_ref[i] = jnp.where(row < cap, own[i * SLOT : (i + 1) * SLOT, :], flat).astype(BF)


def grads_kernel(
    scale, cnt_ref, qg_ref, kv_ref, st_ref, out_ref, qg_pad, kv_pad, turn
):
    nz, cap, hd = qg_ref.shape[0], qg_ref.shape[1], qg_ref.shape[2] // 2
    n = nz * SLOT
    qg = padded(qg_pad, qg_ref, 0, 2 * hd)
    kv = padded(kv_pad, kv_ref, 0, 2 * hd)
    q, g, k, v = qg[:, :hd], qg[:, hd:], kv[:, :hd], kv[:, hd:]
    chunks = -(-n // WIDE)
    logs, deltas = [], []
    for i in range(nz):
        r = st_ref[i].astype(F32)[cap:]
        line = [jnp.concatenate([r[4 * j + s : 4 * j + s + 1] for j in range(chunks)], axis=1) for s in range(4)]
        logs.append(line[0] + line[1])
        deltas.append(line[2] + line[3])
    top = functools.reduce(jnp.maximum, logs)
    weights = [jnp.exp(x - top) for x in logs]
    total = functools.reduce(jnp.add, weights)
    shares = [w / total for w in weights]
    delta = functools.reduce(jnp.add, [w * d for w, d in zip(shares, deltas)])
    log_total = (top + jnp.log(total))[:, :n]
    width = chunks * WIDE
    lines = shares + [d - delta for d in deltas] + [jnp.zeros((128 - 2 * nz, width), F32)]
    turn[...] = jnp.concatenate(lines, axis=0).T
    delta = delta[:, :n]
    mine = turn[pl.ds(pl.multiple_of(lax.axis_index("z") * SLOT, SLOT), SLOT), :]
    grad_q = jnp.zeros((cap, hd), F32)
    for i in range(nz):
        a = st_ref[i, :cap, :hd].astype(F32)
        b = st_ref[i, :cap, hd:].astype(F32)
        grad_q = grad_q + mine[:cap, i : i + 1] * (a + mine[:cap, nz + i : nz + i + 1] * b)
    order_q, order_k = orders(cnt_ref, nz, 1)
    allowed = order_k <= order_q
    s = mm(k, q, NT) * scale
    p = jnp.exp(jnp.where(allowed, s - log_total, NEG))
    ds = (p * (mm(v, g, NT) - delta)).astype(BF)
    grad_k = (mm(ds, q) * scale).astype(BF).reshape(NY, SLOT, hd)
    grad_v = mm(p.astype(BF), g).astype(BF).reshape(NY, SLOT, hd)
    grad_q = grad_q.astype(BF)
    for i in range(NY):
        out_ref[i, :, :hd] = grad_k[i, :cap]
        out_ref[i, :, hd : 2 * hd] = grad_v[i, :cap]
        out_ref[i, :, 2 * hd :] = grad_q


def rows_kernel(back_ref, kv_ref, wq_ref, wk_ref, wv_ref, g_ref, t_ref, x_pad, q_pad):
    heads, cap, cols = g_ref.shape
    hd = wq_ref.shape[1]
    kv = jnp.zeros((cap, 2 * hd), F32)
    for i in range(NY):
        kv = kv + back_ref[i, :, : 2 * hd].astype(F32)
    qkv = jnp.concatenate([back_ref[lax.axis_index("y"), :, 2 * hd :], kv.astype(BF)], axis=1)
    x = padded(x_pad, kv_ref, 2 * hd, kv_ref.shape[2])
    grad_q = padded(q_pad, back_ref, 2 * hd, 3 * hd)
    t_ref[...] = mm(x, grad_q, TN).reshape(t_ref.shape).astype(BF)
    for c in range(heads):
        part = pl.ds(c * cols, cols)
        w = jnp.concatenate([wq_ref[part, :], wk_ref[part, :], wv_ref[part, :]], axis=1)
        g_ref[c] = mm(qkv, w, NT).astype(BF)


def finish_kernel(cnt_ref, sel_ref, g_ref, t_ref, h_out, w_out, pad_ref, ready, sems):
    heads, cap, cols = g_ref.shape
    toks = h_out.shape[0]
    block = lax.axis_index("z") * NY + lax.axis_index("y")
    column = sel_ref[...].astype(F32).T
    row = lax.broadcasted_iota(jnp.int32, (SLOT, 1), 0)
    target = []
    for h in range(heads):
        at = column[:SLOT, h : h + 1].astype(jnp.int32)
        target.append(jnp.where(row < cnt_ref[h, block], at, -1))
    target = jnp.concatenate(target, axis=0)
    lane = lax.broadcasted_iota(jnp.int32, (heads * SLOT, toks), 1)
    hit = jnp.where(lane == target, 1.0, 0.0).astype(BF)
    grads = padded(pad_ref, g_ref, 0, cols)
    leave = []
    for i in range(cols // WIDE):
        at = pl.ds(i * WIDE, WIDE)
        ready[:, at] = mm(hit, grads[:, i * WIDE : (i + 1) * WIDE], TN).astype(BF)
        leave.append(pltpu.make_async_copy(ready.at[:, at], h_out.at[:, at], sems.at[i]))
        leave[i].start()
    w_out[...] = jnp.sum(t_ref[...].astype(F32), axis=0)
    for copy in leave:
        copy.wait()


def body(hidden, upstream, w_query, w_key, w_value, w_output, selected, select_count):
    nz, heads = lax.axis_size("z"), lax.axis_size("head")
    toks, cols = hidden.shape
    hd = w_query.shape[2]
    cap = selected.shape[1] // (nz * NY)
    scale = hd ** (-0.5)
    sds = jax.ShapeDtypeStruct

    def swap(x, axis):
        return lax.all_to_all(x, axis, split_axis=0, concat_axis=0, tiled=True)

    picked, mine = call(
        pick_kernel,
        (sds((heads, 2 * cap, cols), BF), sds((heads, 128), jnp.int32)),
        (selected, hidden, upstream),
        [HBM] * 3,
        [
            pltpu.VMEM((2 * toks, cols), BF),
            pltpu.VMEM((heads, 2 * cap, cols), BF),
            pltpu.VMEM((heads, WIDE), jnp.int32),
            pltpu.SemaphoreType.DMA((7,)),
            pltpu.SemaphoreType.DMA((min(heads, 4),)),
        ],
        limit=54 << 20,
        flops=20000000000,
        out_specs=(HBM, VMEM),
    )
    rows = swap(picked, "head")
    piece = heads * cols // NY
    to_z, to_y = call(
        functools.partial(project_kernel, nz),
        (sds((1, cap, 2 * hd), BF), sds((NY, cap, 2 * hd + piece), BF)),
        (select_count, rows, w_query[0], w_key[0], w_value[0], w_output[0]),
        [HBM] + [VMEM] * 5,
        [
            pltpu.VMEM((2 * cap, hd), F32),
            pltpu.VMEM((NY, cap, 2 * hd + piece), BF),
            pltpu.VMEM(select_count.shape, jnp.int32),
            pltpu.SemaphoreType.DMA((2 * NY,)),
            pltpu.SemaphoreType.DMA,
        ],
        out_specs=(VMEM, HBM),
    )
    count, to_z, to_y = lax.optimization_barrier((select_count, to_z, to_y))
    qg = lax.all_gather(to_z, "z", axis=0, tiled=True)
    kv = swap(to_y, "y")
    pads = [pltpu.VMEM((nz, SLOT, 2 * hd), BF), pltpu.VMEM((NY, SLOT, 2 * hd), BF)]
    part = call(
        functools.partial(partial_kernel, scale),
        sds((nz, SLOT, 2 * hd), BF),
        (count, qg, kv),
        [SMEM] + [VMEM] * 2,
        pads,
    )
    joined = swap(part, "z")
    grads = call(
        functools.partial(grads_kernel, scale),
        sds((NY, cap, 3 * hd), BF),
        (count, qg, kv, joined),
        [SMEM] + [VMEM] * 3,
        pads + [pltpu.VMEM((-(-nz * SLOT // WIDE) * WIDE, 128), F32)],
    )
    back = swap(grads, "y")
    grad_rows, weight_terms = call(
        rows_kernel,
        (sds((heads, cap, cols), BF), sds((nz, piece // nz, hd), BF)),
        (back, kv, w_query[0], w_key[0], w_value[0]),
        [VMEM] * 5,
        [pltpu.VMEM((NY, SLOT, piece), BF), pltpu.VMEM((NY, SLOT, hd), BF)],
    )
    terms = swap(weight_terms, "z")
    grad_rows, terms = lax.optimization_barrier((grad_rows, terms))
    returned = swap(grad_rows, "head")
    grad_hidden, grad_query = call(
        finish_kernel,
        (sds((toks, cols), BF), sds((piece // nz, hd), F32)),
        (count, mine, returned, terms),
        [SMEM] + [VMEM] * 3,
        [
            pltpu.VMEM((heads, SLOT, cols), BF),
            pltpu.VMEM((toks, cols), BF),
            pltpu.SemaphoreType.DMA((cols // WIDE,)),
        ],
        out_specs=(HBM, VMEM),
    )
    return grad_hidden, grad_query[None]


def solution(mesh):
    seq, heads = mesh.devices.shape
    fine = Mesh(mesh.devices.reshape(seq // NY, NY, heads), ("z", "y", "head"))
    both = ("z", "y")
    weight = P("head", None, None)
    in_specs = (P(both, "head"), P(both, "head"), weight, weight, weight, weight, P(), P())
    out_specs = (P(both, "head"), P("head", both, None))
    return jax.shard_map(body, mesh=fine, in_specs=in_specs, out_specs=out_specs, check_vma=False)
```
